512 devices in a mesh: hid: 16 (over y, x), inter: 32 (over z, core).
Axes of the slice: x: 4, y: 4, z: 16, core: 2. Of those that a mesh axis runs over, the one named last changes fastest.
Arguments:
- tokens: bfloat16 [256, 16384], P('inter', 'hid'), may hold values from -6 to 6
- gate_words: float32 [4096, 40960], P('hid', 'inter'), may hold values from 0 to 65535, as said below
- gate_scales: bfloat16 [128, 40960], P('hid', 'inter'), may hold values from 0.00077819824 to 0.003112793
- gate_zeros: int32 [128, 40960], P('hid', 'inter'), may hold values from 7 to 9
- up_words: float32 [4096, 40960], P('hid', 'inter'), may hold values from 0 to 65535, as said below
- up_scales: bfloat16 [128, 40960], P('hid', 'inter'), may hold values from 0.00077819824 to 0.003112793
- up_zeros: int32 [128, 40960], P('hid', 'inter'), may hold values from 7 to 9
- sign_bits: int32 [40960], P('inter'), may hold values 0 or 1
- down_words: float32 [10240, 16384], P('inter', 'hid'), may hold values from 0 to 65535, as said below
- down_scales: bfloat16 [320, 16384], P('inter', 'hid'), may hold values from 0.00049209595 to 0.0019683838
- down_zeros: int32 [320, 16384], P('inter', 'hid'), may hold values from 7 to 9
Outputs:
- mixed: bfloat16 [256, 16384], P('inter', 'hid')
The draws below stay inside these ranges and needn't reach their ends.
Inputs may be any that keep to these rules, and one draw needn't show every extreme that they name: `gate_words`: each word is a whole number holding four 4-bit codes, the k-th in the base-16 digit k. `up_words`: each word is a whole number holding four 4-bit codes, the k-th in the base-16 digit k. `down_words`: each word is a whole number holding four 4-bit codes, the k-th in the base-16 digit k.
All inputs are finite; a program needn't handle non-finite values. No bound on the sum of `sign_bits` on one device may be relied on, other than what follows from the above.
Results may differ from the reference program's by a relative error of at most 0.0067.
Values may be sent and summed in bfloat16 or wider, within the bound.
A program may use at most 64 MiB of HBM per device.

```python
import math
import jax
import jax.numpy as jnp
from jax import lax

D = 16384
FF = 40960
TOKENS = 256
N_HID = 16
N_INTER = 32


def draw_gate_words(key, part):
    key = jax.random.fold_in(key, 11)
    return jax.random.randint(key, (D // 4, FF), 0, 65536).astype(jnp.float32)


def draw_up_words(key, part):
    key = jax.random.fold_in(key, 12)
    return jax.random.randint(key, (D // 4, FF), 0, 65536).astype(jnp.float32)


def draw_down_words(key, part):
    key = jax.random.fold_in(key, 13)
    return jax.random.randint(key, (FF // 4, D), 0, 65536).astype(jnp.float32)


def plant(entries, rng, least, high):
    extent = entries.shape
    place = [jax.random.randint(jax.random.fold_in(rng, axis), (), 0, extent[axis]) for axis in range(len(extent))]
    entries = entries.at[tuple(place)].set(least)
    longest = extent.index(max(extent))
    place[longest] = (place[longest] + 1) % extent[longest]
    return entries.at[tuple(place)].set(high)


def levels(stream_key, shape, split, smallest, high):
    gain, own = 1.0, jax.random.fold_in(stream_key, 6)
    for axis_at, shards_of in split:
        heights = jnp.exp(jax.random.uniform(jax.random.fold_in(own, axis_at), (shards_of,), jnp.float32, smallest / len(split), high / len(split)))
        gain = gain * jnp.repeat(heights, shape[axis_at] // shards_of).reshape([-1 if axis == axis_at else 1 for axis in range(len(shape))])
    return gain


def scatter_about(key, dims, spread, bound, cuts=(), held_as=jnp.bfloat16):
    array = spread * jax.random.normal(key, dims, jnp.float32)
    if cuts:
        array = array * levels(key, dims, cuts, -0.22, 0.18)
    return jnp.clip(array, -bound, bound).astype(held_as)


def setup_inputs(seed: int = 0) -> dict:
    keys = jax.random.split(jax.random.key(seed), 12)
    tokens = scatter_about(keys[0], (TOKENS, D), 1.0, 6.0, ((0, 32), (1, 16)))
    gate_words = draw_gate_words(jax.random.fold_in(keys[11], 71), 0)
    gate_scales = jnp.clip(jnp.exp(math.log(0.003112793) - 1.3862944 * jax.random.uniform(keys[2], (D // 128, FF), jnp.float32) ** levels(keys[2], (D // 128, FF), ((0, 16), (1, 32)), -0.2, 0.2)), 0.00077819824, 0.003112793).astype(jnp.bfloat16)
    gate_zeros = plant(jax.random.randint(keys[3], (D // 128, FF), 7, 10), jax.random.fold_in(keys[3], 1), 7, 9).astype(jnp.int32)
    up_words = draw_up_words(jax.random.fold_in(keys[11], 71), 0)
    up_scales = jnp.clip(jnp.exp(math.log(0.003112793) - 1.3862944 * jax.random.uniform(keys[5], (D // 128, FF), jnp.float32) ** levels(keys[5], (D // 128, FF), ((0, 16), (1, 32)), -0.2, 0.2)), 0.00077819824, 0.003112793).astype(jnp.bfloat16)
    up_zeros = plant(jax.random.randint(keys[6], (D // 128, FF), 7, 10), jax.random.fold_in(keys[6], 1), 7, 9).astype(jnp.int32)
    sign_bits = plant((jax.random.randint(keys[7], (FF,), 0, 2) < 1).astype(jnp.int32), jax.random.fold_in(keys[7], 1), 0, 1)
    down_words = draw_down_words(jax.random.fold_in(keys[11], 71), 0)
    down_scales = jnp.clip(jnp.exp(math.log(0.0019683838) - 1.3862944 * jax.random.uniform(keys[9], (FF // 128, D), jnp.float32) ** levels(keys[9], (FF // 128, D), ((0, 32), (1, 16)), -0.2, 0.2)), 0.00049209595, 0.0019683838).astype(jnp.bfloat16)
    down_zeros = plant(jax.random.randint(keys[10], (FF // 128, D), 7, 10), jax.random.fold_in(keys[10], 1), 7, 9).astype(jnp.int32)
    return dict(tokens=tokens, gate_words=gate_words, gate_scales=gate_scales, gate_zeros=gate_zeros, up_words=up_words, up_scales=up_scales, up_zeros=up_zeros, sign_bits=sign_bits, down_words=down_words, down_scales=down_scales, down_zeros=down_zeros)


def unpack_codes(packed):
    pieces = []
    for k in range(4):
        lower = jnp.floor(packed / float(16 ** k))
        higher = jnp.floor(packed / float(16 ** (k + 1)))
        pieces.append(lower - 16.0 * higher)
    return jnp.stack(pieces, axis=1).reshape(packed.shape[0] * 4, packed.shape[1])

def dequantize(packed, scales, zero_points):
    code_values = unpack_codes(packed)
    groups = code_values.shape[0] // 128
    grouped = code_values.reshape(groups, 128, code_values.shape[1])
    weight = (grouped - zero_points[:, None, :].astype(grouped.dtype)) * scales[:, None, :].astype(grouped.dtype)
    return weight.reshape(groups * 128, code_values.shape[1]).astype(jnp.bfloat16)

def sylvester(order):
    index_col = jnp.arange(order, dtype=jnp.int32)
    parity = jnp.zeros((order, order), jnp.int32)
    for bit_pos in range(order.bit_length() - 1):
        both = jnp.bitwise_and(jnp.right_shift(index_col[:, None], bit_pos), jnp.right_shift(index_col[None, :], bit_pos))
        parity = parity + jnp.bitwise_and(both, 1)
    return (1 - 2 * jnp.bitwise_and(parity, 1)).astype(jnp.float32)

def reference(tokens, gate_words, gate_scales, gate_zeros, up_words, up_scales, up_zeros, sign_bits, down_words, down_scales, down_zeros):
    width = D // N_HID

    def accumulate(totals, shard):
        inputs = lax.dynamic_slice_in_dim(tokens, shard * width, width, 1)
        results = []
        for packed, scales, zero_points in ((gate_words, gate_scales, gate_zeros), (up_words, up_scales, up_zeros)):
            weight = dequantize(lax.dynamic_slice_in_dim(packed, shard * (width // 4), width // 4, 0), lax.dynamic_slice_in_dim(scales, shard * (width // 128), width // 128, 0), lax.dynamic_slice_in_dim(zero_points, shard * (width // 128), width // 128, 0))
            results.append(jnp.dot(inputs, weight, preferred_element_type=jnp.float32))
        return ((totals[0] + results[0], totals[1] + results[1]), None)
    empty = jnp.zeros((TOKENS, FF), jnp.float32)
    (gate, up), unused = lax.scan(accumulate, (empty, empty), jnp.arange(N_HID, dtype=jnp.int32))
    hidden = jax.nn.silu(gate) * up
    signed = hidden * (1 - 2 * sign_bits).astype(jnp.float32)[None, :]
    local = FF // N_INTER
    lattice = signed.reshape(TOKENS, N_INTER, local // 128, 128)
    lattice = jnp.einsum('ij,tjbk->tibk', sylvester(N_INTER), lattice, precision=lax.Precision.HIGHEST)
    lattice = jnp.einsum('tibk,kl->tibl', lattice, sylvester(128), precision=lax.Precision.HIGHEST)
    rotated = (lattice.reshape(TOKENS, FF) / math.sqrt(N_INTER * 128)).astype(jnp.bfloat16)

    def project(total, shard):
        weight = dequantize(lax.dynamic_slice_in_dim(down_words, shard * (local // 4), local // 4, 0), lax.dynamic_slice_in_dim(down_scales, shard * (local // 128), local // 128, 0), lax.dynamic_slice_in_dim(down_zeros, shard * (local // 128), local // 128, 0))
        piece = lax.dynamic_slice_in_dim(rotated, shard * local, local, 1)
        return (total + jnp.dot(piece, weight, preferred_element_type=jnp.float32), None)
    mixed, unused = lax.scan(project, jnp.zeros((TOKENS, D), jnp.float32), jnp.arange(N_INTER, dtype=jnp.int32))
    return mixed.astype(jnp.bfloat16)
```

```python
import functools

import jax
import jax.numpy as jnp
from jax import lax
from jax.experimental import pallas as pl
from jax.experimental.pallas import tpu as pltpu
from jax.sharding import PartitionSpec as P

MESH = pl.DeviceIdType.MESH
F32 = jnp.float32
BF16 = jnp.bfloat16
NH, NZ, NJ, NB = 16, 16, 32, 10


def slot_of(d):
    return (d + 3) % 16


def wait_bytes(view, sem):
    pltpu.make_async_copy(view, view, sem).wait()


def loop(lo, hi, fn):
    def step(i, carry):
        fn(i)
        return carry

    lax.fori_loop(lo, hi, step, 0)


def dequantized(words, zero, scale):
    w = words.astype(jnp.int32)
    planes = []
    for k in range(4):
        d = jnp.right_shift(w, 4 * k) if k else w
        if k < 3:
            d = jnp.bitwise_and(d, 15)
        planes.append(((d.astype(F32) - zero) * scale).astype(BF16))
    return planes


def kernel(
    tok, gw_hbm, gs, gz, uw_hbm, us, uz, sb, dw_hbm, ds, dz,
    out,
    gw, uw, dw, gsf, gzf, usf, uzf, dsf, dzf, sgn,
    W, Wd, X, L, S, B, U, C1, C2, R2, R, Lown, Loth, EXs, EXr, Pown, SB2, SB8, G, G8, T4, Fr,
    w_sem, as1, as2, asc, ar, arc, bs, br, c1s, c1r, c2s, c2r, dsd, drv, e1s, e1r, e2s, e2r, e3s, e3r,
):
    h = lax.axis_index("hid")
    j = lax.axis_index("inter")
    z = lax.div(j, 2)
    c = lax.rem(j, 2)
    oc = 1 - c

    def zdev(d):
        return (h, 2 * lax.rem(z + d + 16, 16) + c)

    other = (h, 2 * z + oc)

    def rcopy(src, dst, ss, rs, dev):
        return pltpu.make_async_remote_copy(
            src_ref=src, dst_ref=dst, send_sem=ss, recv_sem=rs, device_id=dev, device_id_type=MESH
        )

    loads = [
        pltpu.make_async_copy(gw_hbm, gw, w_sem.at[0]),
        pltpu.make_async_copy(uw_hbm, uw, w_sem.at[1]),
        pltpu.make_async_copy(dw_hbm, dw, w_sem.at[2]),
    ]
    for cp in loads:
        cp.start()

    bar = pltpu.get_barrier_semaphore()
    loop(1, NJ, lambda i: pl.semaphore_signal(
        bar, inc=1, device_id=(h, lax.rem(j + i, NJ)), device_id_type=MESH))
    loop(1, NH, lambda i: pl.semaphore_signal(
        bar, inc=1, device_id=(lax.rem(h + i, NH), j), device_id_type=MESH))

    rows = lax.broadcasted_iota(jnp.int32, (128, 128), 0)
    cols = lax.broadcasted_iota(jnp.int32, (128, 128), 1)
    place = 32 * jnp.bitwise_and(rows, 3) + jnp.right_shift(rows, 2)
    shuffle = jnp.where(place == cols, 1.0, 0.0).astype(BF16)
    for g in range(4):
        both = [
            jnp.dot(tok[:, 512 * u + 128 * g:512 * u + 128 * g + 128], shuffle, preferred_element_type=F32)
            for u in range(2)
        ]
        X[3, c, g] = jnp.concatenate(both, axis=0).astype(BF16)

    gsf[...] = gs[...].astype(F32)
    usf[...] = us[...].astype(F32)
    gzf[...] = gz[...].astype(F32)
    uzf[...] = uz[...].astype(F32)
    dsv, dzv, sgv = ds[...].astype(F32), dz[...].astype(F32), (1 - 2 * sb[...]).astype(F32)
    for b in range(NB):
        dsf[b], dzf[b], sgn[b] = dsv[b:b + 1], dzv[b:b + 1], sgv[b:b + 1]

    pl.semaphore_wait(bar, NJ - 1 + NH - 1)

    first = (4, -4, 1, -1, 2, -2, 3, -3)
    stage1 = [
        rcopy(X.at[3, c], X.at[slot_of(-e), c], as1.at[k], ar.at[slot_of(-e)], zdev(e))
        for k, e in enumerate(first)
    ]
    for cp in stage1:
        cp.start()

    def to_core(s):
        return rcopy(X.at[s, c], X.at[s, c], asc, arc.at[s // 8], other)

    to_core(3).start()

    def arrived(s):
        wait_bytes(X.at[s, c], ar.at[s])

    def dequant_gu(b):
        at = pl.ds(pl.multiple_of(b * 128, 128), 128)
        for words, zf, sf, lane in ((gw, gzf, gsf, 0), (uw, uzf, usf, 128)):
            for g in range(8):
                planes = dequantized(words[32 * g:32 * g + 32, at], zf[g:g + 1, at], sf[g:g + 1, at])
                for k in range(4):
                    W[b, 128 * g + 32 * k:128 * g + 32 * k + 32, lane:lane + 128] = planes[k]

    loads[0].wait()
    loads[1].wait()
    loop(0, 4, dequant_gu)

    stage2 = []
    for way in (1, -1):
        s = slot_of(-4 * way)
        arrived(s)
        for e in (1, 2, 3):
            to = slot_of(-(4 + e) * way)
            stage2.append(rcopy(X.at[s, c], X.at[to, c], as2.at[len(stage2)], ar.at[to], zdev(e * way)))
        half = 0 if way == 1 else 1
        stage2.append(rcopy(
            X.at[s, c, pl.ds(2 * half, 2)], X.at[slot_of(8), c, pl.ds(2 * half, 2)],
            as2.at[len(stage2)], ar.at[16 + half], zdev(4 * way)))
        for cp in stage2[-4:]:
            cp.start()
    to_core(slot_of(4)).start()
    to_core(slot_of(-4)).start()
    for e in (1, -1, 2, -2, 3, -3):
        arrived(slot_of(e))
        to_core(slot_of(e)).start()

    loop(4, NB, dequant_gu)

    for e in (5, -5, 6, -6, 7, -7):
        arrived(slot_of(e))
        to_core(slot_of(e)).start()
    for half in range(2):
        wait_bytes(X.at[slot_of(8), c, pl.ds(2 * half, 2)], ar.at[16 + half])
    to_core(slot_of(8)).start()

    for part in range(2):
        wait_bytes(X.at[pl.ds(8 * part, 8), oc], arc.at[part])

        def lay(s, part=part):
            at = pl.ds(pl.multiple_of(16 * s, 16), 16)
            for g in range(4):
                t0 = X[8 * part + s, 0, g].astype(F32)
                t1 = X[8 * part + s, 1, g].astype(F32)
                L[at, 128 * g:128 * g + 128] = jnp.concatenate([t0[:8], t1[:8]], axis=0).astype(BF16)
                L[at, 512 + 128 * g:640 + 128 * g] = jnp.concatenate([t0[8:], t1[8:]], axis=0).astype(BF16)

        loop(0, 8, lay)

        def product(b, part=part):
            v = jnp.dot(L[...], W[b], preferred_element_type=F32).astype(BF16)
            for s in range(8):
                r = 10 * s + b
                for u in range(2):
                    S[part, lax.div(r, 16), lax.rem(r, 16), u] = v[16 * s:16 * s + 16, 128 * u:128 * u + 128]

        loop(0, NB, product)

        n0 = 10 * lax.rem(z + 13 + 8 * part, 16)

        def send(p, part=part, n0=n0):
            y = lax.rem(lax.div(h, 4) + lax.div(p, 4), 4)
            x = lax.rem(lax.rem(h, 4) + lax.rem(p, 4), 4)
            to = 4 * y + x
            r0 = lax.rem(to - n0 + 160, 16)
            rcopy(S.at[part, :, r0], B.at[part, h], bs.at[part], br.at[part], (to, j)).start()

        loop(1, NH, send)
        B[part, h] = S[part, :, lax.rem(h - n0 + 160, 16)]

    loads[2].wait()

    def dequant_d(b):
        at = pl.ds(pl.multiple_of(b * 32, 32), 32)
        for q in range(8):
            lanes = slice(128 * q, 128 * q + 128)
            planes = dequantized(dw[at, lanes], dzf[b, :, lanes], dsf[b, :, lanes])
            for k in range(4):
                to = pl.ds(pl.multiple_of(b * 128 + 32 * k, 32), 32)
                Wd[q // 2, to, 128 * (q % 2):128 * (q % 2) + 128] = planes[k]

    loop(0, NB, dequant_d)

    for cp in stage1 + stage2:
        cp.wait_send()
    wait_bytes(X.at[:, c], asc)

    for part in range(2):
        wait_bytes(B.at[part, pl.ds(0, NH - 1)], br.at[part])
        n0 = 10 * lax.rem(z + 13 + 8 * part, 16)
        r0 = lax.rem(h - n0 + 160, 16)

        def unit(q, part=part, n0=n0, r0=r0):
            n = lax.rem(n0 + r0 + 16 * q, 160)
            total = B[part, 0, q].astype(F32)
            for s in range(1, NH):
                total = total + B[part, s, q].astype(F32)
            gate, up = total[0], total[1]
            hidden = gate / (1.0 + jnp.exp(-gate)) * up
            U[lax.div(n, 16)] = (hidden * sgn[lax.rem(n, 10)]).astype(BF16)

        loop(0, 5, unit)

    def collect(m):
        owner = 3 * m + 1

        @pl.when(owner != j)
        def _():
            rcopy(U.at[m], C1.at[j], c1s.at[m], c1r, (h, owner)).start()

        @pl.when(owner == j)
        def _():
            C1[j] = U[m]

    loop(0, NB, collect)

    owns = jnp.logical_and(lax.rem(j, 3) == 1, j <= 28)
    mine = lax.div(j, 3)

    @pl.when(owns)
    def _():
        turned = 4 * jnp.bitwise_and(cols, 31) + jnp.right_shift(cols, 5)
        common = jnp.bitwise_and(rows, turned)
        odd = jnp.zeros_like(common)
        for bit in range(7):
            odd = jnp.bitwise_xor(odd, jnp.right_shift(common, bit))
        factor = (1 - 2 * jnp.bitwise_and(odd, 1)).astype(F32).astype(BF16)
        wait_bytes(C1.at[pl.ds(0, NJ - 1)], c1r)
        vals = [jnp.dot(C1[i], factor, preferred_element_type=F32) for i in range(NJ)]
        step = 1
        while step < NJ:
            vals = [
                vals[i] + vals[i ^ step] if not i & step else vals[i ^ step] - vals[i] for i in range(NJ)
            ]
            step *= 2
        for i in range(NJ):
            C2[i] = (vals[i] * (1.0 / 64.0)).astype(BF16)

        def back(p):
            i = lax.rem(j + p, NJ)
            rcopy(C2.at[i], R2.at[mine], c2s, c2r, (h, i)).start()

        loop(1, NJ, back)
        R2[mine] = C2[j]
        wait_bytes(R2.at[pl.ds(0, NB - 1)], c2r)

    @pl.when(jnp.logical_not(owns))
    def _():
        wait_bytes(R2.at[pl.ds(0, NB)], c2r)

    def spread(p):
        y = lax.rem(lax.div(h, 4) + lax.div(p, 4), 4)
        x = lax.rem(lax.rem(h, 4) + lax.rem(p, 4), 4)
        rcopy(R2, R.at[:, h], dsd, drv, (4 * y + x, j)).start()

    loop(1, NH, spread)
    for m in range(NB):
        R[m, h] = R2[m]

    for part in range(2):
        wait_bytes(S.at[part, :, pl.ds(0, NH - 1)], bs.at[part])

    def collected(m):
        @pl.when(3 * m + 1 != j)
        def _():
            wait_bytes(U.at[m], c1s.at[m])

    loop(0, NB, collected)

    @pl.when(owns)
    def _():
        wait_bytes(C2.at[pl.ds(0, NJ - 1)], c2s)

    wait_bytes(R.at[:, pl.ds(0, NH - 1)], drv)

    def split(a):
        at = pl.ds(pl.multiple_of(16 * a, 16), 16)
        for b in range(NB):
            n = 20 * a + b
            t0 = R[lax.div(n, 16), lax.rem(n, 16)].astype(F32)
            t1 = R[lax.div(n + 10, 16), lax.rem(n + 10, 16)].astype(F32)
            low = jnp.concatenate([t0[:8], t1[:8]], axis=0)
            high = jnp.concatenate([t0[8:], t1[8:]], axis=0)
            lanes = slice(128 * b, 128 * b + 128)
            Lown[at, lanes] = jnp.where(c == 0, low, high).astype(BF16)
            Loth[at, lanes] = jnp.where(c == 0, high, low).astype(BF16)

    loop(0, 8, split)

    def pair(lhs, i):
        lo = jnp.dot(lhs[...], Wd[i], preferred_element_type=F32).reshape(NZ, 8, 256)
        hi = jnp.dot(lhs[...], Wd[2 + i], preferred_element_type=F32).reshape(NZ, 8, 256)
        return jnp.concatenate([lo, hi], axis=1)

    def for_other(i):
        EXs[i] = pair(Loth, i).astype(BF16)
        rcopy(EXs.at[i], EXr.at[i], e1s.at[i], e1r.at[i], other).start()

    loop(0, 2, for_other)

    def for_own(i):
        Pown[i] = pair(Lown, i)

    loop(0, 2, for_own)

    for i in range(2):
        wait_bytes(EXr.at[i], e1r.at[i])

    def block(d, i):
        at = lax.rem(z + d + 16, 16)
        return Pown[i, at] + EXr[i, at].astype(F32)

    SB8[0] = block(8, 0).astype(BF16)
    SB8[1] = block(8, 1).astype(BF16)
    sends = [
        rcopy(SB8.at[0], G8.at[0], e2s.at[6], e2r.at[6], zdev(4)),
        rcopy(SB8.at[1], G8.at[1], e2s.at[7], e2r.at[7], zdev(-4)),
    ]
    sends[0].start()
    sends[1].start()
    for e in (3, 2, 1):
        for way in (1, -1):
            k = e - 1 if way == 1 else 2 + e
            for i in range(2):
                SB2[k, 0, i] = block(e * way, i).astype(BF16)
                SB2[k, 1, i] = block((e + 4) * way, i).astype(BF16)
            cp = rcopy(SB2.at[k], G.at[k], e2s.at[k], e2r.at[k], zdev(e * way))
            cp.start()
            sends.append(cp)

    for k in range(6):
        wait_bytes(G.at[k], e2r.at[k])
    for k in range(2):
        wait_bytes(G8.at[k], e2r.at[6 + k])
    for side, way in ((0, 1), (1, -1)):
        for i in range(2):
            total = block(4 * way, i)
            for k in range(3):
                total = total + G[3 * side + k, 1, i].astype(F32)
            if i == side:
                total = total + G8[side].astype(F32)
            T4[side, i] = total.astype(BF16)
        cp = rcopy(T4.at[side], Fr.at[side], e3s.at[side], e3r.at[side], zdev(4 * way))
        cp.start()
        sends.append(cp)

    totals = []
    for i in range(2):
        total = block(0, i)
        for k in range(6):
            total = total + G[k, 0, i].astype(F32)
        totals.append(total)
    for cp in sends:
        cp.wait_send()
    for i in range(2):
        wait_bytes(EXs.at[i], e1s.at[i])
    wait_bytes(R.at[:, pl.ds(0, NH - 1)], dsd)
    for side in range(2):
        wait_bytes(Fr.at[side], e3r.at[side])
    for i in range(2):
        total = totals[i] + Fr[0, i].astype(F32) + Fr[1, i].astype(F32)
        out[:, 256 * i:256 * i + 256] = total[:8].astype(BF16)
        out[:, 512 + 256 * i:768 + 256 * i] = total[8:].astype(BF16)


def body(tok, gw, gs, gz, uw, us, uz, sb, dw, ds, dz):
    vmem = pl.BlockSpec(memory_space=pltpu.VMEM)
    hbm = pl.BlockSpec(memory_space=pl.ANY)
    V = pltpu.VMEM
    D = pltpu.SemaphoreType.DMA
    return pl.pallas_call(
        kernel,
        out_shape=jax.ShapeDtypeStruct((8, 1024), BF16),
        in_specs=[vmem, hbm, vmem, vmem, hbm, vmem, vmem, vmem, hbm, vmem, vmem],
        out_specs=vmem,
        scratch_shapes=[
            V((256, 1280), F32), V((256, 1280), F32), V((320, 1024), F32),
            V((8, 1280), F32), V((8, 1280), F32), V((8, 1280), F32), V((8, 1280), F32),
            V((10, 1, 1024), F32), V((10, 1, 1024), F32), V((10, 1, 128), F32),
            V((10, 1024, 256), BF16),
            V((4, 1280, 256), BF16),
            V((16, 2, 4, 16, 128), BF16),
            V((128, 1024), BF16),
            V((2, 5, 16, 2, 16, 128), BF16),
            V((2, 16, 5, 2, 16, 128), BF16),
            V((10, 16, 128), BF16),
            V((32, 16, 128), BF16),
            V((32, 16, 128), BF16),
            V((10, 16, 128), BF16),
            V((10, 16, 16, 128), BF16),
            V((128, 1280), BF16), V((128, 1280), BF16),
            V((2, 16, 16, 256), BF16), V((2, 16, 16, 256), BF16),
            V((2, 16, 16, 256), F32),
            V((6, 2, 2, 16, 256), BF16), V((2, 16, 256), BF16),
            V((6, 2, 2, 16, 256), BF16), V((2, 16, 256), BF16),
            V((2, 2, 16, 256), BF16), V((2, 2, 16, 256), BF16),
            D((3,)), D((8,)), D((8,)), D, D((18,)), D((2,)), D((2,)), D((2,)),
            D((10,)), D, D, D, D, D, D((2,)), D((2,)), D((8,)), D((8,)), D((2,)), D((2,)),
        ],
        compiler_params=pltpu.CompilerParams(
            collective_id=0, has_side_effects=True, vmem_limit_bytes=48 * 1024 * 1024
        ),
        name="rotated_ffn",
    )(tok, gw, gs, gz, uw, us, uz, sb.reshape(10, 128), dw, ds, dz)


def solution(mesh):
    in_specs = (
        P("inter", "hid"),
        P("hid", "inter"),
        P("hid", "inter"),
        P("hid", "inter"),
        P("hid", "inter"),
        P("hid", "inter"),
        P("hid", "inter"),
        P("inter"),
        P("inter", "hid"),
        P("inter", "hid"),
        P("inter", "hid"),
    )
    return jax.shard_map(
        body, mesh=mesh, in_specs=in_specs, out_specs=P("inter", "hid"), check_vma=False
    )
```

```python
import functools

import jax
import jax.numpy as jnp
from jax import lax
from jax.experimental import pallas as pl
from jax.experimental.pallas import tpu as pltpu
from jax.sharding import PartitionSpec as P

MESH = pl.DeviceIdType.MESH
F32 = jnp.float32
BF16 = jnp.bfloat16
NH, NZ, NJ, NB = 16, 16, 32, 10


def slot_of(d):
    return (d + 3) % 16


def wait_bytes(view, sem):
    pltpu.make_async_copy(view, view, sem).wait()


def loop(lo, hi, fn):
    def step(i, carry):
        fn(i)
        return carry

    lax.fori_loop(lo, hi, step, 0)


def dequantized(words, zero, scale):
    w = words.astype(jnp.int32)
    planes = []
    for k in range(4):
        d = jnp.right_shift(w, 4 * k) if k else w
        if k < 3:
            d = jnp.bitwise_and(d, 15)
        planes.append(((d.astype(F32) - zero) * scale).astype(BF16))
    return planes


def kernel(
    *refs,
):
    inputs, out, scratch = refs[:11], refs[11], refs[12:]
    held = scratch[:11]
    tok, gw, gs, gz, uw, us, uz, sb, dw, ds, dz = held
    (
    gsf, gzf, usf, uzf, dsf, dzf, sgn,
    W, Wd, X, L, S, B, U, C1, C2, R2, R, Lown, Loth, EXs, EXr, Pown, SB2, SB8, G, G8, T4, Fr,
    w_sem, as1, as2, asc, ar, arc, bs, br, c1s, c1r, c2s, c2r, dsd, drv, e1s, e1r, e2s, e2r, e8s, e8r, e3s, e3r,
    ) = scratch[11:]
    h = lax.axis_index("hid")
    j = lax.axis_index("inter")
    z = lax.div(j, 2)
    c = lax.rem(j, 2)
    oc = 1 - c

    def zdev(d):
        return (h, 2 * lax.rem(z + d + 16, 16) + c)

    other = (h, 2 * z + oc)

    def rcopy(src, dst, ss, rs, dev):
        return pltpu.make_async_remote_copy(
            src_ref=src, dst_ref=dst, send_sem=ss, recv_sem=rs, device_id=dev, device_id_type=MESH
        )

    near = (4, -4, 1, -1, 2, -2, 3, -3)
    bar = pltpu.get_barrier_semaphore()
    for d in near:
        pl.semaphore_signal(bar, inc=1, device_id=zdev(d), device_id_type=MESH)
    pl.semaphore_signal(bar, inc=1, device_id=other, device_id_type=MESH)
    loop(1, NH, lambda i: pl.semaphore_signal(
        bar, inc=1, device_id=(lax.rem(h + i, NH), j), device_id_type=MESH))

    loads = [pltpu.make_async_copy(inputs[i], held[i], w_sem.at[i]) for i in range(11)]
    for i in (0, 1, 4, 2, 3, 5, 6, 8, 7, 9, 10):
        loads[i].start()

    rows = lax.broadcasted_iota(jnp.int32, (128, 128), 0)
    cols = lax.broadcasted_iota(jnp.int32, (128, 128), 1)
    place = 32 * jnp.bitwise_and(rows, 3) + jnp.right_shift(rows, 2)
    shuffle = jnp.where(place == cols, 1.0, 0.0).astype(BF16)
    loads[0].wait()
    for g in range(4):
        both = [
            jnp.dot(tok[:, 512 * u + 128 * g:512 * u + 128 * g + 128], shuffle, preferred_element_type=F32)
            for u in range(2)
        ]
        X[3, c, g] = jnp.concatenate(both, axis=0).astype(BF16)

    pl.semaphore_wait(bar, len(near) + 1 + NH - 1)

    stage1 = [
        rcopy(X.at[3, c], X.at[slot_of(-e), c], as1.at[k], ar.at[slot_of(-e)], zdev(e))
        for k, e in enumerate(near)
    ]
    for cp in stage1:
        cp.start()

    def to_core(s):
        return rcopy(X.at[s, c], X.at[s, c], asc, arc.at[s // 8], other)

    to_core(3).start()

    def arrived(s):
        wait_bytes(X.at[s, c], ar.at[s])

    def dequant_gu(b):
        at = pl.ds(pl.multiple_of(b * 128, 128), 128)
        for words, zf, sf, lane in ((gw, gzf, gsf, 0), (uw, uzf, usf, 128)):
            for g in range(8):
                planes = dequantized(words[32 * g:32 * g + 32, at], zf[g:g + 1, at], sf[g:g + 1, at])
                for k in range(4):
                    W[b, 128 * g + 32 * k:128 * g + 32 * k + 32, lane:lane + 128] = planes[k]

    for i in (1, 2, 3, 4, 5, 6):
        loads[i].wait()
    gsf[...] = gs[...].astype(F32)
    usf[...] = us[...].astype(F32)
    gzf[...] = gz[...].astype(F32)
    uzf[...] = uz[...].astype(F32)
    loop(0, NB, dequant_gu)

    for i in (7, 8, 9, 10):
        loads[i].wait()
    dsv, dzv, sgv = ds[...].astype(F32), dz[...].astype(F32), (1 - 2 * sb[...]).astype(F32)
    for b in range(NB):
        dsf[b], dzf[b], sgn[b] = dsv[b:b + 1], dzv[b:b + 1], sgv[b:b + 1]

    def dequant_d(b):
        at = pl.ds(pl.multiple_of(b * 32, 32), 32)
        for q in range(8):
            lanes = slice(128 * q, 128 * q + 128)
            planes = dequantized(dw[at, lanes], dzf[b, :, lanes], dsf[b, :, lanes])
            for k in range(4):
                to = pl.ds(pl.multiple_of(b * 128 + 32 * k, 32), 32)
                Wd[q // 2, to, 128 * (q % 2):128 * (q % 2) + 128] = planes[k]

    loop(0, NB, dequant_d)

    stage2 = []
    for way in (1, -1):
        s = slot_of(-4 * way)
        arrived(s)
        for e in (1, 2, 3):
            to = slot_of(-(4 + e) * way)
            stage2.append(rcopy(X.at[s, c], X.at[to, c], as2.at[len(stage2)], ar.at[to], zdev(e * way)))
        half = 0 if way == 1 else 1
        stage2.append(rcopy(
            X.at[s, c, pl.ds(2 * half, 2)], X.at[slot_of(8), c, pl.ds(2 * half, 2)],
            as2.at[len(stage2)], ar.at[16 + half], zdev(4 * way)))
        for cp in stage2[-4:]:
            cp.start()
    to_core(slot_of(4)).start()
    for e in (1, -1, 2, -2, 3, -3):
        arrived(slot_of(e))
        to_core(slot_of(e)).start()
    to_core(slot_of(-4)).start()

    for part in range(2):
        if part == 1:
            for e in (5, -5, 6, -6, 7, -7):
                arrived(slot_of(e))
                to_core(slot_of(e)).start()
            for half in range(2):
                wait_bytes(X.at[slot_of(8), c, pl.ds(2 * half, 2)], ar.at[16 + half])
            to_core(slot_of(8)).start()
        wait_bytes(X.at[pl.ds(8 * part, 8), oc], arc.at[part])

        def lay(s, part=part):
            at = pl.ds(pl.multiple_of(16 * s, 16), 16)
            for g in range(4):
                t0 = X[8 * part + s, 0, g].astype(F32)
                t1 = X[8 * part + s, 1, g].astype(F32)
                L[at, 128 * g:128 * g + 128] = jnp.concatenate([t0[:8], t1[:8]], axis=0).astype(BF16)
                L[at, 512 + 128 * g:640 + 128 * g] = jnp.concatenate([t0[8:], t1[8:]], axis=0).astype(BF16)

        loop(0, 8, lay)

        def product(b, part=part):
            v = jnp.dot(L[...], W[b], preferred_element_type=F32).astype(BF16)
            for s in range(8):
                r = 10 * s + b
                for u in range(2):
                    S[part, lax.div(r, 16), lax.rem(r, 16), u] = v[16 * s:16 * s + 16, 128 * u:128 * u + 128]

        loop(0, NB, product)

        n0 = 10 * lax.rem(z + 13 + 8 * part, 16)

        def send(p, part=part, n0=n0):
            y = lax.rem(lax.div(h, 4) + lax.div(p, 4), 4)
            x = lax.rem(lax.rem(h, 4) + lax.rem(p, 4), 4)
            to = 4 * y + x
            r0 = lax.rem(to - n0 + 160, 16)
            rcopy(S.at[part, :, r0], B.at[part, h], bs.at[part], br.at[part], (to, j)).start()

        loop(1, NH, send)
        B[part, h] = S[part, :, lax.rem(h - n0 + 160, 16)]

    for cp in stage1 + stage2:
        cp.wait_send()
    wait_bytes(X.at[:, c], asc)

    def owner_of(m, side):
        return 8 * lax.div(m, 5) + lax.rem(m, 5) + 16 * side

    def collect(m):
        for side in range(2):
            owner = owner_of(m, side)

            @pl.when(owner != j)
            def _():
                rcopy(U.at[m], C1.at[j], c1s.at[2 * m + side], c1r, (h, owner)).start()

            @pl.when(owner == j)
            def _():
                C1[j] = U[m]

    for part in range(2):
        wait_bytes(B.at[part, pl.ds(0, NH - 1)], br.at[part])
        n0 = 10 * lax.rem(z + 13 + 8 * part, 16)
        r0 = lax.rem(h - n0 + 160, 16)

        def unit(q, part=part, n0=n0, r0=r0):
            n = lax.rem(n0 + r0 + 16 * q, 160)
            total = B[part, 0, q].astype(F32)
            for s in range(1, NH):
                total = total + B[part, s, q].astype(F32)
            gate, up = total[0], total[1]
            hidden = gate / (1.0 + jnp.exp(-gate)) * up
            m = lax.div(n, 16)
            U[m] = (hidden * sgn[lax.rem(n, 10)]).astype(BF16)
            collect(m)

        loop(0, 5, unit)

    owns = lax.rem(j, 8) < 5
    mine = 5 * lax.div(lax.rem(j, 16), 8) + lax.rem(j, 8)

    @pl.when(owns)
    def _():
        turned = 4 * jnp.bitwise_and(cols, 31) + jnp.right_shift(cols, 5)
        common = jnp.bitwise_and(rows, turned)
        odd = jnp.zeros_like(common)
        for bit in range(7):
            odd = jnp.bitwise_xor(odd, jnp.right_shift(common, bit))
        factor = (1 - 2 * jnp.bitwise_and(odd, 1)).astype(F32).astype(BF16)
        wait_bytes(C1.at[pl.ds(0, NJ - 1)], c1r)
        vals = [jnp.dot(C1[i], factor, preferred_element_type=F32) for i in range(NJ)]
        step = 1
        while step < NJ:
            vals = [
                vals[i] + vals[i ^ step] if not i & step else vals[i ^ step] - vals[i] for i in range(NJ)
            ]
            step *= 2
        for i in range(NJ):
            C2[i] = (vals[i] * (1.0 / 64.0)).astype(BF16)

        def back(q):
            i = 2 * lax.rem(z + lax.div(q, 2) + 12, 16) + lax.rem(q, 2)

            @pl.when(i != j)
            def _():
                rcopy(C2.at[i], R2.at[mine], c2s, c2r, (h, i)).start()

        loop(0, 16, back)
        R2[mine] = C2[j]
        wait_bytes(R2.at[pl.ds(0, NB - 1)], c2r)

    @pl.when(jnp.logical_not(owns))
    def _():
        wait_bytes(R2.at[pl.ds(0, NB)], c2r)

    def spread(p):
        y = lax.rem(lax.div(h, 4) + lax.div(p, 4), 4)
        x = lax.rem(lax.rem(h, 4) + lax.rem(p, 4), 4)
        rcopy(R2, R.at[:, h], dsd, drv, (4 * y + x, j)).start()

    loop(1, NH, spread)
    for m in range(NB):
        R[m, h] = R2[m]

    for part in range(2):
        wait_bytes(S.at[part, :, pl.ds(0, NH - 1)], bs.at[part])

    def collected(m):
        for side in range(2):
            @pl.when(owner_of(m, side) != j)
            def _():
                wait_bytes(U.at[m], c1s.at[2 * m + side])

    loop(0, NB, collected)

    @pl.when(owns)
    def _():
        wait_bytes(C2.at[pl.ds(0, 15)], c2s)

    wait_bytes(R.at[:, pl.ds(0, NH - 1)], drv)

    def split(a):
        at = pl.ds(pl.multiple_of(16 * a, 16), 16)
        for b in range(NB):
            n = 20 * a + b
            t0 = R[lax.div(n, 16), lax.rem(n, 16)].astype(F32)
            t1 = R[lax.div(n + 10, 16), lax.rem(n + 10, 16)].astype(F32)
            low = jnp.concatenate([t0[:8], t1[:8]], axis=0)
            high = jnp.concatenate([t0[8:], t1[8:]], axis=0)
            lanes = slice(128 * b, 128 * b + 128)
            Lown[at, lanes] = jnp.where(c == 0, low, high).astype(BF16)
            Loth[at, lanes] = jnp.where(c == 0, high, low).astype(BF16)

    loop(0, 8, split)

    def pair(lhs, i):
        lo = jnp.dot(lhs[...], Wd[i], preferred_element_type=F32).reshape(NZ, 8, 256)
        hi = jnp.dot(lhs[...], Wd[2 + i], preferred_element_type=F32).reshape(NZ, 8, 256)
        return jnp.concatenate([lo, hi], axis=1)

    def for_other(i):
        EXs[i] = pair(Loth, i).astype(BF16)
        rcopy(EXs.at[i], EXr.at[i], e1s.at[i], e1r.at[i], other).start()

    loop(0, 2, for_other)

    def block(d, i):
        at = lax.rem(z + d + 16, 16)
        return Pown[i, at] + EXr[i, at].astype(F32)

    sends = []
    for i in range(2):
        Pown[i] = pair(Lown, i)
        wait_bytes(EXr.at[i], e1r.at[i])
        SB8[i] = block(8, i).astype(BF16)
        cp = rcopy(SB8.at[i], G8.at[i], e8s.at[i], e8r.at[i], zdev(4 if i == 0 else -4))
        cp.start()
        sends.append(cp)
        for e in (3, 2, 1):
            for way in (1, -1):
                k = e - 1 if way == 1 else 2 + e
                SB2[i, k, 0] = block(e * way, i).astype(BF16)
                SB2[i, k, 1] = block((e + 4) * way, i).astype(BF16)
                cp = rcopy(SB2.at[i, k], G.at[i, k], e2s.at[i, k], e2r.at[i, k], zdev(e * way))
                cp.start()
                sends.append(cp)

    for i in range(2):
        for k in (2, 5, 1, 4, 0, 3):
            wait_bytes(G.at[i, k], e2r.at[i, k])
        wait_bytes(G8.at[i], e8r.at[i])
        for side, way in ((0, 1), (1, -1)):
            total = block(4 * way, i)
            for k in range(3):
                total = total + G[i, 3 * side + k, 1].astype(F32)
            if i == side:
                total = total + G8[i].astype(F32)
            T4[i, side] = total.astype(BF16)
            cp = rcopy(T4.at[i, side], Fr.at[i, side], e3s.at[i, side], e3r.at[i, side], zdev(4 * way))
            cp.start()
            sends.append(cp)

    totals = []
    for i in range(2):
        total = block(0, i)
        for k in range(6):
            total = total + G[i, k, 0].astype(F32)
        totals.append(total)
    for cp in sends:
        cp.wait_send()
    for i in range(2):
        wait_bytes(EXs.at[i], e1s.at[i])
    wait_bytes(R.at[:, pl.ds(0, NH - 1)], dsd)
    for i in range(2):
        for side in range(2):
            wait_bytes(Fr.at[i, side], e3r.at[i, side])
        total = totals[i] + Fr[i, 0].astype(F32) + Fr[i, 1].astype(F32)
        out[:, 256 * i:256 * i + 256] = total[:8].astype(BF16)
        out[:, 512 + 256 * i:768 + 256 * i] = total[8:].astype(BF16)


def body(tok, gw, gs, gz, uw, us, uz, sb, dw, ds, dz):
    vmem = pl.BlockSpec(memory_space=pltpu.VMEM)
    hbm = pl.BlockSpec(memory_space=pl.ANY)
    V = pltpu.VMEM
    D = pltpu.SemaphoreType.DMA
    operands = (tok, gw, gs, gz, uw, us, uz, sb.reshape(10, 128), dw, ds, dz)
    return pl.pallas_call(
        kernel,
        out_shape=jax.ShapeDtypeStruct((8, 1024), BF16),
        in_specs=[hbm] * 11,
        out_specs=vmem,
        scratch_shapes=[
            *[V(x.shape, x.dtype) for x in operands],
            V((8, 1280), F32), V((8, 1280), F32), V((8, 1280), F32), V((8, 1280), F32),
            V((10, 1, 1024), F32), V((10, 1, 1024), F32), V((10, 1, 128), F32),
            V((10, 1024, 256), BF16),
            V((4, 1280, 256), BF16),
            V((16, 2, 4, 16, 128), BF16),
            V((128, 1024), BF16),
            V((2, 5, 16, 2, 16, 128), BF16),
            V((2, 16, 5, 2, 16, 128), BF16),
            V((10, 16, 128), BF16),
            V((32, 16, 128), BF16),
            V((32, 16, 128), BF16),
            V((10, 16, 128), BF16),
            V((10, 16, 16, 128), BF16),
            V((128, 1280), BF16), V((128, 1280), BF16),
            V((2, 16, 16, 256), BF16), V((2, 16, 16, 256), BF16),
            V((2, 16, 16, 256), F32),
            V((2, 6, 2, 16, 256), BF16), V((2, 16, 256), BF16),
            V((2, 6, 2, 16, 256), BF16), V((2, 16, 256), BF16),
            V((2, 2, 16, 256), BF16), V((2, 2, 16, 256), BF16),
            D((11,)), D((8,)), D((8,)), D, D((18,)), D((2,)), D((2,)), D((2,)),
            D((20,)), D, D, D, D, D, D((2,)), D((2,)), D((2, 6)), D((2, 6)), D((2,)), D((2,)), D((2, 2)), D((2, 2)),
        ],
        compiler_params=pltpu.CompilerParams(
            collective_id=0, has_side_effects=True, vmem_limit_bytes=60 * 1024 * 1024
        ),
        name="rotated_ffn",
    )(*operands)


def solution(mesh):
    in_specs = (
        P("inter", "hid"),
        P("hid", "inter"),
        P("hid", "inter"),
        P("hid", "inter"),
        P("hid", "inter"),
        P("hid", "inter"),
        P("hid", "inter"),
        P("inter"),
        P("inter", "hid"),
        P("inter", "hid"),
        P("inter", "hid"),
    )
    return jax.shard_map(
        body, mesh=mesh, in_specs=in_specs, out_specs=P("inter", "hid"), check_vma=False
    )
```

```python
import functools

import jax
import jax.numpy as jnp
from jax import lax
from jax.experimental import pallas as pl
from jax.experimental.pallas import tpu as pltpu
from jax.sharding import PartitionSpec as P

MESH = pl.DeviceIdType.MESH
F32 = jnp.float32
BF16 = jnp.bfloat16
NH, NZ, NJ, NB = 16, 16, 32, 10


def slot_of(d):
    return (d + 3) % 16


def wait_bytes(view, sem):
    pltpu.make_async_copy(view, view, sem).wait()


def loop(lo, hi, fn):
    def step(i, carry):
        fn(i)
        return carry

    lax.fori_loop(lo, hi, step, 0)


def dequantized(words, zero, scale):
    w = words.astype(jnp.int32)
    planes = []
    for k in range(4):
        d = jnp.right_shift(w, 4 * k) if k else w
        if k < 3:
            d = jnp.bitwise_and(d, 15)
        planes.append(((d.astype(F32) - zero) * scale).astype(BF16))
    return planes


def kernel(
    *refs,
):
    inputs, out, scratch = refs[:11], refs[11], refs[12:]
    held = scratch[:11]
    tok, gw, gs, gz, uw, us, uz, sb, dw, ds, dz = held
    (
    gsf, gzf, usf, uzf, dsf, dzf, sgn,
    W, Wd, X, L, S, B, U, C1, C2, R2, R, Lown, Loth, EXs, EXr, Pown, SB2, SB8, G, G8, T4, Fr,
    w_sem, as1, as2, asc, ar, arc, bs, br, c1s, c1r, c2s, c2r, dsd, drv, e1s, e1r, e2s, e2r, e8s, e8r, e3s, e3r,
    ) = scratch[11:]
    h = lax.axis_index("hid")
    j = lax.axis_index("inter")
    z = lax.div(j, 2)
    c = lax.rem(j, 2)
    oc = 1 - c

    def zdev(d):
        return (h, 2 * lax.rem(z + d + 16, 16) + c)

    other = (h, 2 * z + oc)

    def rcopy(src, dst, ss, rs, dev):
        return pltpu.make_async_remote_copy(
            src_ref=src, dst_ref=dst, send_sem=ss, recv_sem=rs, device_id=dev, device_id_type=MESH
        )

    near = (4, -4, 1, -1, 2, -2, 3, -3)
    bar = pltpu.get_barrier_semaphore()
    for d in near:
        pl.semaphore_signal(bar, inc=1, device_id=zdev(d), device_id_type=MESH)
    pl.semaphore_signal(bar, inc=1, device_id=other, device_id_type=MESH)
    loop(1, NH, lambda i: pl.semaphore_signal(
        bar, inc=1, device_id=(lax.rem(h + i, NH), j), device_id_type=MESH))

    loads = [pltpu.make_async_copy(inputs[i], held[i], w_sem.at[i]) for i in range(11)]
    for i in (0, 1, 4, 2, 3, 5, 6, 8, 7, 9, 10):
        loads[i].start()

    rows = lax.broadcasted_iota(jnp.int32, (128, 128), 0)
    cols = lax.broadcasted_iota(jnp.int32, (128, 128), 1)
    place = 32 * jnp.bitwise_and(rows, 3) + jnp.right_shift(rows, 2)
    shuffle = jnp.where(place == cols, 1.0, 0.0).astype(BF16)
    def dequant_gu(b):
        at = pl.ds(pl.multiple_of(b * 128, 128), 128)
        for words, zf, sf, lane in ((gw, gzf, gsf, 0), (uw, uzf, usf, 128)):
            for g in range(8):
                planes = dequantized(words[32 * g:32 * g + 32, at], zf[g:g + 1, at], sf[g:g + 1, at])
                for k in range(4):
                    W[b, 128 * g + 32 * k:128 * g + 32 * k + 32, lane:lane + 128] = planes[k]

    loads[0].wait()
    for g in range(4):
        both = [
            jnp.dot(tok[:, 512 * u + 128 * g:512 * u + 128 * g + 128], shuffle, preferred_element_type=F32)
            for u in range(2)
        ]
        X[3, c, g] = jnp.concatenate(both, axis=0).astype(BF16)

    for i in (1, 2, 3, 4, 5, 6):
        loads[i].wait()
    gsf[...] = gs[...].astype(F32)
    usf[...] = us[...].astype(F32)
    gzf[...] = gz[...].astype(F32)
    uzf[...] = uz[...].astype(F32)
    loop(0, NB, dequant_gu)

    pl.semaphore_wait(bar, len(near) + 1 + NH - 1)

    stage1 = [
        rcopy(X.at[3, c], X.at[slot_of(-e), c], as1.at[k], ar.at[slot_of(-e)], zdev(e))
        for k, e in enumerate(near)
    ]
    for cp in stage1:
        cp.start()

    def to_core(s):
        return rcopy(X.at[s, c], X.at[s, c], asc, arc.at[s], other)

    to_core(3).start()

    def arrived(s):
        wait_bytes(X.at[s, c], ar.at[s])

    stage2 = []
    for way in (1, -1):
        s = slot_of(-4 * way)
        arrived(s)
        for e in (1, 2, 3):
            to = slot_of(-(4 + e) * way)
            stage2.append(rcopy(X.at[s, c], X.at[to, c], as2.at[len(stage2)], ar.at[to], zdev(e * way)))
        half = 0 if way == 1 else 1
        stage2.append(rcopy(
            X.at[s, c, pl.ds(2 * half, 2)], X.at[slot_of(8), c, pl.ds(2 * half, 2)],
            as2.at[len(stage2)], ar.at[16 + half], zdev(4 * way)))
        for cp in stage2[-4:]:
            cp.start()
    to_core(slot_of(4)).start()
    for e in (1, -1, 2, -2, 3, -3):
        arrived(slot_of(e))
        to_core(slot_of(e)).start()
    to_core(slot_of(-4)).start()

    def products(slots):
        for s in slots:
            wait_bytes(X.at[s, oc], arc.at[s])
        for i, s in enumerate(slots):
            for g in range(4):
                t0, t1 = X[s, 0, g].astype(F32), X[s, 1, g].astype(F32)
                at = slice(16 * i, 16 * i + 16)
                L[at, 128 * g:128 * g + 128] = jnp.concatenate([t0[:8], t1[:8]], axis=0).astype(BF16)
                L[at, 512 + 128 * g:640 + 128 * g] = jnp.concatenate([t0[8:], t1[8:]], axis=0).astype(BF16)

        def product(b):
            v = jnp.dot(L[:16 * len(slots)], W[b], preferred_element_type=F32).astype(BF16)
            for i, s in enumerate(slots):
                n = 10 * lax.rem(z + 13 + s, 16) + b
                m, to = lax.div(n, 16), lax.rem(n, 16)
                for u in range(2):
                    S[s, b, u] = v[16 * i:16 * i + 16, 128 * u:128 * u + 128]

                @pl.when(to != h)
                def _(s=s, m=m, to=to):
                    rcopy(S.at[s, b], B.at[m, h], bs, br.at[m], (to, j)).start()

                @pl.when(to == h)
                def _(s=s, m=m):
                    B[m, h] = S[s, b]

        loop(0, NB, product)

    products(range(8))
    for e in (5, -5, 6):
        arrived(slot_of(e))
        to_core(slot_of(e)).start()
    products((8, 9, 14, 15))
    for e in (-6, 7, -7):
        arrived(slot_of(e))
        to_core(slot_of(e)).start()
    for half in range(2):
        wait_bytes(X.at[slot_of(8), c, pl.ds(2 * half, 2)], ar.at[16 + half])
    to_core(slot_of(8)).start()
    products((10, 11, 12, 13))

    for i in (7, 8, 9, 10):
        loads[i].wait()
    dsv, dzv, sgv = ds[...].astype(F32), dz[...].astype(F32), (1 - 2 * sb[...]).astype(F32)
    for b in range(NB):
        dsf[b], dzf[b], sgn[b] = dsv[b:b + 1], dzv[b:b + 1], sgv[b:b + 1]

    def dequant_d(b):
        at = pl.ds(pl.multiple_of(b * 32, 32), 32)
        for q in range(8):
            lanes = slice(128 * q, 128 * q + 128)
            planes = dequantized(dw[at, lanes], dzf[b, :, lanes], dsf[b, :, lanes])
            for k in range(4):
                to = pl.ds(pl.multiple_of(b * 128 + 32 * k, 32), 32)
                Wd[q // 2, to, 128 * (q % 2):128 * (q % 2) + 128] = planes[k]

    loop(0, NB, dequant_d)

    for cp in stage1 + stage2:
        cp.wait_send()
    wait_bytes(X.at[:, c], asc)

    def owner_of(m, side):
        return 8 * lax.div(m, 5) + lax.rem(m, 5) + 16 * side

    def collect(m):
        for side in range(2):
            owner = owner_of(m, side)

            @pl.when(owner != j)
            def _():
                rcopy(U.at[m], C1.at[j], c1s.at[2 * m + side], c1r, (h, owner)).start()

            @pl.when(owner == j)
            def _():
                C1[j] = U[m]

    n0 = 10 * lax.rem(z + 13, 16)
    n0 = n0 + lax.rem(h - n0 + 160, 16)

    def unit(k):
        n = lax.rem(n0 + 16 * k, 160)
        m = lax.div(n, 16)
        wait_bytes(B.at[m, pl.ds(0, NH - 1)], br.at[m])
        total = B[m, 0].astype(F32)
        for s in range(1, NH):
            total = total + B[m, s].astype(F32)
        gate, up = total[0], total[1]
        hidden = gate / (1.0 + jnp.exp(-gate)) * up
        U[m] = (hidden * sgn[lax.rem(n, 10)]).astype(BF16)
        collect(m)

    loop(0, 5, unit)
    loop(0, 5, lambda i: unit(5 + (4 * lax.rem(i, 2)) + lax.div(i, 2) * (1 - 2 * lax.rem(i, 2))))

    owns = lax.rem(j, 8) < 5
    mine = 5 * lax.div(lax.rem(j, 16), 8) + lax.rem(j, 8)

    @pl.when(owns)
    def _():
        turned = 4 * jnp.bitwise_and(cols, 31) + jnp.right_shift(cols, 5)
        common = jnp.bitwise_and(rows, turned)
        odd = jnp.zeros_like(common)
        for bit in range(7):
            odd = jnp.bitwise_xor(odd, jnp.right_shift(common, bit))
        factor = (1 - 2 * jnp.bitwise_and(odd, 1)).astype(F32).astype(BF16)
        wait_bytes(C1.at[pl.ds(0, NJ - 1)], c1r)
        vals = [jnp.dot(C1[i], factor, preferred_element_type=F32) for i in range(NJ)]
        step = 1
        while step < NJ:
            vals = [
                vals[i] + vals[i ^ step] if not i & step else vals[i ^ step] - vals[i] for i in range(NJ)
            ]
            step *= 2
        for i in range(NJ):
            C2[i] = (vals[i] * (1.0 / 64.0)).astype(BF16)

        def back(q):
            i = 2 * lax.rem(z + lax.div(q, 2) + 12, 16) + lax.rem(q, 2)

            @pl.when(i != j)
            def _():
                rcopy(C2.at[i], R2.at[mine], c2s, c2r.at[mine], (h, i)).start()

        loop(0, 16, back)
        R2[mine] = C2[j]

    start = lax.div(5 * lax.rem(z, 8) + 2, 4)
    for step in (0, 1, 9, 2, 8, 3, 7, 4, 6, 5):
        m = lax.rem(start + step, NB)

        @pl.when(jnp.logical_not(jnp.logical_and(owns, m == mine)))
        def _(m=m):
            wait_bytes(R2.at[m], c2r.at[m])

        def spread(p, m=m):
            y = lax.rem(lax.div(h, 4) + lax.div(p, 4), 4)
            x = lax.rem(lax.rem(h, 4) + lax.rem(p, 4), 4)
            rcopy(R2.at[m], R.at[m, h], dsd, drv, (4 * y + x, j)).start()

        loop(1, NH, spread)
        R[m, h] = R2[m]

    wait_bytes(S.at[pl.ds(0, 15)], bs)

    def collected(m):
        for side in range(2):
            @pl.when(owner_of(m, side) != j)
            def _():
                wait_bytes(U.at[m], c1s.at[2 * m + side])

    loop(0, NB, collected)

    @pl.when(owns)
    def _():
        wait_bytes(C2.at[pl.ds(0, 15)], c2s)

    wait_bytes(R.at[:, pl.ds(0, NH - 1)], drv)

    def split(a):
        at = pl.ds(pl.multiple_of(16 * a, 16), 16)
        for b in range(NB):
            n = 20 * a + b
            t0 = R[lax.div(n, 16), lax.rem(n, 16)].astype(F32)
            t1 = R[lax.div(n + 10, 16), lax.rem(n + 10, 16)].astype(F32)
            low = jnp.concatenate([t0[:8], t1[:8]], axis=0)
            high = jnp.concatenate([t0[8:], t1[8:]], axis=0)
            lanes = slice(128 * b, 128 * b + 128)
            Lown[at, lanes] = jnp.where(c == 0, low, high).astype(BF16)
            Loth[at, lanes] = jnp.where(c == 0, high, low).astype(BF16)

    loop(0, 8, split)

    def pair(lhs, i):
        lo = jnp.dot(lhs[...], Wd[i], preferred_element_type=F32).reshape(NZ, 8, 256)
        hi = jnp.dot(lhs[...], Wd[2 + i], preferred_element_type=F32).reshape(NZ, 8, 256)
        return jnp.concatenate([lo, hi], axis=1)

    def for_other(i):
        EXs[i] = pair(Loth, i).astype(BF16)
        rcopy(EXs.at[i], EXr.at[i], e1s.at[i], e1r.at[i], other).start()

    loop(0, 2, for_other)

    def block(d, i):
        at = lax.rem(z + d + 16, 16)
        return Pown[i, at] + EXr[i, at].astype(F32)

    sends = []
    for i in range(2):
        Pown[i] = pair(Lown, i)
        wait_bytes(EXr.at[i], e1r.at[i])
        SB8[i] = block(8, i).astype(BF16)
        cp = rcopy(SB8.at[i], G8.at[i], e8s.at[i], e8r.at[i], zdev(4 if i == 0 else -4))
        cp.start()
        sends.append(cp)
        for e in (3, 2, 1):
            for way in (1, -1):
                k = e - 1 if way == 1 else 2 + e
                SB2[i, k, 0] = block(e * way, i).astype(BF16)
                SB2[i, k, 1] = block((e + 4) * way, i).astype(BF16)
                cp = rcopy(SB2.at[i, k], G.at[i, k], e2s.at[i, k], e2r.at[i, k], zdev(e * way))
                cp.start()
                sends.append(cp)

    for i in range(2):
        for k in (2, 5, 1, 4, 0, 3):
            wait_bytes(G.at[i, k], e2r.at[i, k])
        wait_bytes(G8.at[i], e8r.at[i])
        for side, way in ((0, 1), (1, -1)):
            total = block(4 * way, i)
            for k in range(3):
                total = total + G[i, 3 * side + k, 1].astype(F32)
            if i == side:
                total = total + G8[i].astype(F32)
            T4[i, side] = total.astype(BF16)
            cp = rcopy(T4.at[i, side], Fr.at[i, side], e3s.at[i, side], e3r.at[i, side], zdev(4 * way))
            cp.start()
            sends.append(cp)

    totals = []
    for i in range(2):
        total = block(0, i)
        for k in range(6):
            total = total + G[i, k, 0].astype(F32)
        totals.append(total)
    for cp in sends:
        cp.wait_send()
    for i in range(2):
        wait_bytes(EXs.at[i], e1s.at[i])
    wait_bytes(R.at[:, pl.ds(0, NH - 1)], dsd)
    for i in range(2):
        for side in range(2):
            wait_bytes(Fr.at[i, side], e3r.at[i, side])
        total = totals[i] + Fr[i, 0].astype(F32) + Fr[i, 1].astype(F32)
        out[:, 256 * i:256 * i + 256] = total[:8].astype(BF16)
        out[:, 512 + 256 * i:768 + 256 * i] = total[8:].astype(BF16)


def body(tok, gw, gs, gz, uw, us, uz, sb, dw, ds, dz):
    vmem = pl.BlockSpec(memory_space=pltpu.VMEM)
    hbm = pl.BlockSpec(memory_space=pl.ANY)
    V = pltpu.VMEM
    D = pltpu.SemaphoreType.DMA
    operands = (tok, gw, gs, gz, uw, us, uz, sb.reshape(10, 128), dw, ds, dz)
    return pl.pallas_call(
        kernel,
        out_shape=jax.ShapeDtypeStruct((8, 1024), BF16),
        in_specs=[hbm] * 11,
        out_specs=vmem,
        scratch_shapes=[
            *[V(x.shape, x.dtype) for x in operands],
            V((8, 1280), F32), V((8, 1280), F32), V((8, 1280), F32), V((8, 1280), F32),
            V((10, 1, 1024), F32), V((10, 1, 1024), F32), V((10, 1, 128), F32),
            V((10, 1024, 256), BF16),
            V((4, 1280, 256), BF16),
            V((16, 2, 4, 16, 128), BF16),
            V((128, 1024), BF16),
            V((16, 10, 2, 16, 128), BF16),
            V((10, 16, 2, 16, 128), BF16),
            V((10, 16, 128), BF16),
            V((32, 16, 128), BF16),
            V((32, 16, 128), BF16),
            V((10, 16, 128), BF16),
            V((10, 16, 16, 128), BF16),
            V((128, 1280), BF16), V((128, 1280), BF16),
            V((2, 16, 16, 256), BF16), V((2, 16, 16, 256), BF16),
            V((2, 16, 16, 256), F32),
            V((2, 6, 2, 16, 256), BF16), V((2, 16, 256), BF16),
            V((2, 6, 2, 16, 256), BF16), V((2, 16, 256), BF16),
            V((2, 2, 16, 256), BF16), V((2, 2, 16, 256), BF16),
            D((11,)), D((8,)), D((8,)), D, D((18,)), D((16,)), D, D((10,)),
            D((20,)), D, D, D((10,)), D, D, D((2,)), D((2,)), D((2, 6)), D((2, 6)), D((2,)), D((2,)), D((2, 2)), D((2, 2)),
        ],
        compiler_params=pltpu.CompilerParams(
            collective_id=0, has_side_effects=True, vmem_limit_bytes=60 * 1024 * 1024
        ),
        name="rotated_ffn",
    )(*operands)


def solution(mesh):
    in_specs = (
        P("inter", "hid"),
        P("hid", "inter"),
        P("hid", "inter"),
        P("hid", "inter"),
        P("hid", "inter"),
        P("hid", "inter"),
        P("hid", "inter"),
        P("inter"),
        P("inter", "hid"),
        P("inter", "hid"),
        P("inter", "hid"),
    )
    return jax.shard_map(
        body, mesh=mesh, in_specs=in_specs, out_specs=P("inter", "hid"), check_vma=False
    )
```

```python
import functools

import jax
import jax.numpy as jnp
from jax import lax
from jax.experimental import pallas as pl
from jax.experimental.pallas import tpu as pltpu
from jax.sharding import PartitionSpec as P

MESH = pl.DeviceIdType.MESH
F32 = jnp.float32
BF16 = jnp.bfloat16
NH, NZ, NJ, NB = 16, 16, 32, 10


def slot_of(d):
    return (d + 3) % 16


def wait_bytes(view, sem):
    pltpu.make_async_copy(view, view, sem).wait()


def loop(lo, hi, fn):
    def step(i, carry):
        fn(i)
        return carry

    lax.fori_loop(lo, hi, step, 0)


def dequantized(words, zero, scale):
    w = words.astype(jnp.int32)
    planes = []
    for k in range(4):
        d = jnp.right_shift(w, 4 * k) if k else w
        if k < 3:
            d = jnp.bitwise_and(d, 15)
        planes.append(((d.astype(F32) - zero) * scale).astype(BF16))
    return planes


def kernel(
    *refs,
):
    inputs, out, scratch = refs[:11], refs[11], refs[12:]
    held = scratch[:11]
    tok, gw, gs, gz, uw, us, uz, sb, dw, ds, dz = held
    (
    gsf, gzf, usf, uzf, dsf, dzf, sgn,
    W, Wd, X, L, S, B, U, C1, C2, R2, R, Lh, EXs, EXr, Pown, SB, G, T4, Fr,
    w_sem, as1, as2, asc, ar, arc, bs, br, c1s, c1r, c2s, c2r, dsd, drv, e1s, e1r, e2s, e2r, e3s, e3r,
    ) = scratch[11:]
    h = lax.axis_index("hid")
    j = lax.axis_index("inter")
    z = lax.div(j, 2)
    c = lax.rem(j, 2)
    oc = 1 - c

    def zdev(d):
        return (h, 2 * lax.rem(z + d + 16, 16) + c)

    other = (h, 2 * z + oc)

    def rcopy(src, dst, ss, rs, dev):
        return pltpu.make_async_remote_copy(
            src_ref=src, dst_ref=dst, send_sem=ss, recv_sem=rs, device_id=dev, device_id_type=MESH
        )

    near = (4, -4, 3, -3, 2, -2, 1, -1)
    bar = pltpu.get_barrier_semaphore()
    for d in near:
        pl.semaphore_signal(bar, inc=1, device_id=zdev(d), device_id_type=MESH)
    pl.semaphore_signal(bar, inc=1, device_id=other, device_id_type=MESH)
    loop(1, NH, lambda i: pl.semaphore_signal(
        bar, inc=1, device_id=(lax.rem(h + i, NH), j), device_id_type=MESH))

    loads = [pltpu.make_async_copy(inputs[i], held[i], w_sem.at[i]) for i in range(11)]
    for i in (0, 1, 4, 2, 3, 5, 6, 8, 7, 9, 10):
        loads[i].start()

    rows = lax.broadcasted_iota(jnp.int32, (128, 128), 0)
    cols = lax.broadcasted_iota(jnp.int32, (128, 128), 1)
    place = 32 * jnp.bitwise_and(rows, 3) + jnp.right_shift(rows, 2)
    shuffle = jnp.where(place == cols, 1.0, 0.0).astype(BF16)
    def dequant_gu(b):
        at = pl.ds(pl.multiple_of(b * 128, 128), 128)
        for words, zf, sf, lane in ((gw, gzf, gsf, 0), (uw, uzf, usf, 128)):
            for g in range(8):
                planes = dequantized(words[32 * g:32 * g + 32, at], zf[g:g + 1, at], sf[g:g + 1, at])
                for k in range(4):
                    W[b, 128 * g + 32 * k:128 * g + 32 * k + 32, lane:lane + 128] = planes[k]

    loads[0].wait()
    for g in range(4):
        both = [
            jnp.dot(tok[:, 512 * u + 128 * g:512 * u + 128 * g + 128], shuffle, preferred_element_type=F32)
            for u in range(2)
        ]
        X[3, c, g] = jnp.concatenate(both, axis=0).astype(BF16)

    for i in (1, 2, 3, 4, 5, 6):
        loads[i].wait()
    gsf[...] = gs[...].astype(F32)
    usf[...] = us[...].astype(F32)
    gzf[...] = gz[...].astype(F32)
    uzf[...] = uz[...].astype(F32)
    loop(0, NB, dequant_gu)

    pl.semaphore_wait(bar, len(near) + 1 + NH - 1)

    stage1 = [
        rcopy(X.at[3, c], X.at[slot_of(-e), c], as1.at[k], ar.at[slot_of(-e)], zdev(e))
        for k, e in enumerate(near)
    ]
    for cp in stage1:
        cp.start()

    def to_core(s):
        return rcopy(X.at[s, c], X.at[s, c], asc, arc.at[s], other)

    to_core(3).start()

    def arrived(s):
        wait_bytes(X.at[s, c], ar.at[s])

    stage2 = []
    for way in (1, -1):
        s = slot_of(-4 * way)
        arrived(s)
        half = 0 if way == 1 else 1
        stage2.append(rcopy(
            X.at[s, c, pl.ds(2 * half, 2)], X.at[slot_of(8), c, pl.ds(2 * half, 2)],
            as2.at[len(stage2)], ar.at[16 + half], zdev(4 * way)))
        for e in (3, 2, 1):
            to = slot_of(-(4 + e) * way)
            stage2.append(rcopy(X.at[s, c], X.at[to, c], as2.at[len(stage2)], ar.at[to], zdev(e * way)))
        for cp in stage2[-4:]:
            cp.start()
    to_core(slot_of(4)).start()
    for e in (1, -1, 2, -2, 3, -3):
        arrived(slot_of(e))
        to_core(slot_of(e)).start()
    to_core(slot_of(-4)).start()

    def products(slots):
        for s in slots:
            wait_bytes(X.at[s, oc], arc.at[s])
        for i, s in enumerate(slots):
            for g in range(4):
                t0, t1 = X[s, 0, g].astype(F32), X[s, 1, g].astype(F32)
                at = slice(16 * i, 16 * i + 16)
                L[at, 128 * g:128 * g + 128] = jnp.concatenate([t0[:8], t1[:8]], axis=0).astype(BF16)
                L[at, 512 + 128 * g:640 + 128 * g] = jnp.concatenate([t0[8:], t1[8:]], axis=0).astype(BF16)

        def product(b):
            v = jnp.dot(L[:16 * len(slots)], W[b], preferred_element_type=F32).astype(BF16)
            for i, s in enumerate(slots):
                n = 10 * lax.rem(z + 13 + s, 16) + b
                m, to = lax.div(n, 16), lax.rem(n, 16)
                for u in range(2):
                    S[s, b, u] = v[16 * i:16 * i + 16, 128 * u:128 * u + 128]

                @pl.when(to != h)
                def _(s=s, m=m, to=to):
                    rcopy(S.at[s, b], B.at[m, h], bs, br.at[m], (to, j)).start()

                @pl.when(to == h)
                def _(s=s, m=m):
                    B[m, h] = S[s, b]

        loop(0, NB, lambda i: product(lax.rem(i + h, NB)))

    products(range(8))
    for e in (5, -5, 6):
        arrived(slot_of(e))
        to_core(slot_of(e)).start()
    for e in (-6, 7, -7):
        arrived(slot_of(e))
        to_core(slot_of(e)).start()
    for half in range(2):
        wait_bytes(X.at[slot_of(8), c, pl.ds(2 * half, 2)], ar.at[16 + half])
    to_core(slot_of(8)).start()
    products((8, 9, 14, 15))
    products((10, 11, 12, 13))

    for i in (7, 8, 9, 10):
        loads[i].wait()
    dsv, dzv, sgv = ds[...].astype(F32), dz[...].astype(F32), (1 - 2 * sb[...]).astype(F32)
    for b in range(NB):
        dsf[b], dzf[b], sgn[b] = dsv[b:b + 1], dzv[b:b + 1], sgv[b:b + 1]

    def dequant_d(b):
        at = pl.ds(pl.multiple_of(b * 32, 32), 32)
        for q in range(8):
            lanes = slice(128 * q, 128 * q + 128)
            planes = dequantized(dw[at, lanes], dzf[b, :, lanes], dsf[b, :, lanes])
            for k in range(4):
                to = pl.ds(pl.multiple_of(b * 128 + 32 * k, 32), 32)
                Wd[q // 2, to, 128 * (q % 2):128 * (q % 2) + 128] = planes[k]

    loop(0, NB, dequant_d)

    for cp in stage1 + stage2:
        cp.wait_send()
    wait_bytes(X.at[:, c], asc)

    def owner_of(m, side):
        return 8 * lax.div(m, 5) + lax.rem(m, 5) + 16 * side

    def collect(m):
        for side in range(2):
            owner = owner_of(m, side)

            @pl.when(owner != j)
            def _():
                rcopy(U.at[m], C1.at[j], c1s.at[2 * m + side], c1r, (h, owner)).start()

            @pl.when(owner == j)
            def _():
                C1[j] = U[m]

    n0 = 10 * lax.rem(z + 13, 16)
    n0 = n0 + lax.rem(h - n0 + 160, 16)

    def unit(k):
        n = lax.rem(n0 + 16 * k, 160)
        m = lax.div(n, 16)
        wait_bytes(B.at[m, pl.ds(0, NH - 1)], br.at[m])
        total = B[m, 0].astype(F32)
        for s in range(1, NH):
            total = total + B[m, s].astype(F32)
        gate, up = total[0], total[1]
        hidden = gate / (1.0 + jnp.exp(-gate)) * up
        U[m] = (hidden * sgn[lax.rem(n, 10)]).astype(BF16)
        collect(m)

    loop(0, 5, unit)
    loop(0, 5, lambda i: unit(5 + (4 * lax.rem(i, 2)) + lax.div(i, 2) * (1 - 2 * lax.rem(i, 2))))

    owns = lax.rem(j, 8) < 5
    mine = 5 * lax.div(lax.rem(j, 16), 8) + lax.rem(j, 8)

    @pl.when(owns)
    def _():
        turned = 4 * jnp.bitwise_and(cols, 31) + jnp.right_shift(cols, 5)
        common = jnp.bitwise_and(rows, turned)
        odd = jnp.zeros_like(common)
        for bit in range(7):
            odd = jnp.bitwise_xor(odd, jnp.right_shift(common, bit))
        factor = (1 - 2 * jnp.bitwise_and(odd, 1)).astype(F32).astype(BF16)
        wait_bytes(C1.at[pl.ds(0, NJ - 1)], c1r)
        vals = [jnp.dot(C1[i], factor, preferred_element_type=F32) for i in range(NJ)]
        step = 1
        while step < NJ:
            vals = [
                vals[i] + vals[i ^ step] if not i & step else vals[i ^ step] - vals[i] for i in range(NJ)
            ]
            step *= 2
        for i in range(NJ):
            C2[i] = (vals[i] * (1.0 / 64.0)).astype(BF16)

        def back(q):
            d = lax.div(q + 2, 4)
            d = jnp.where(lax.rem(lax.div(q, 2), 2) == 0, d - 4, 4 - d)
            i = 2 * lax.rem(z + d + 16, 16) + lax.rem(q, 2)

            @pl.when(i != j)
            def _():
                rcopy(C2.at[i], R2.at[mine], c2s, c2r.at[mine], (h, i)).start()

        loop(0, 16, back)
        R2[mine] = C2[j]

    first_half = lax.rem(lax.div(z + 1, 4), 2)
    rising = lax.rem(z + 1, 4) < 2
    for step in range(NB):
        half = first_half if step < 5 else 1 - first_half
        m = 5 * half + jnp.where(rising, step % 5, 4 - step % 5)

        @pl.when(jnp.logical_not(jnp.logical_and(owns, m == mine)))
        def _(m=m):
            wait_bytes(R2.at[m], c2r.at[m])

        def spread(p, m=m, half=half):
            y = lax.rem(lax.div(h, 4) + lax.div(p + 10, 4), 4)
            x = lax.rem(h + p + 10, 4)
            rcopy(R2.at[m], R.at[m, h], dsd, drv.at[half], (4 * y + x, j)).start()

        loop(0, 6, spread)
        loop(7, NH, spread)
        R[m, h] = R2[m]

    wait_bytes(S.at[pl.ds(0, 15)], bs)

    def collected(m):
        for side in range(2):
            @pl.when(owner_of(m, side) != j)
            def _():
                wait_bytes(U.at[m], c1s.at[2 * m + side])

    loop(0, NB, collected)

    @pl.when(owns)
    def _():
        wait_bytes(C2.at[pl.ds(0, 15)], c2s)

    def block(at, i):
        return Pown[i, at] + EXr[i, at].astype(F32)

    def chip_at(d):
        return lax.rem(z + d + 16, 16)

    for half in (first_half, 1 - first_half):
        wait_bytes(R.at[pl.ds(5 * half, 5), pl.ds(0, NH - 1)], drv.at[half])

        def split(a, half=half):
            for b in range(NB):
                n = 80 * half + 20 * a + b
                t0 = R[lax.div(n, 16), lax.rem(n, 16)].astype(F32)
                t1 = R[lax.div(n + 10, 16), lax.rem(n + 10, 16)].astype(F32)
                low = jnp.concatenate([t0[:8], t1[:8]], axis=0)
                high = jnp.concatenate([t0[8:], t1[8:]], axis=0)
                lanes = slice(128 * b, 128 * b + 128)
                at = pl.multiple_of(16 * a, 16)
                Lh[pl.ds(at, 16), lanes] = jnp.where(c == 0, high, low).astype(BF16)
                Lh[pl.ds(at + 64, 16), lanes] = jnp.where(c == 0, low, high).astype(BF16)

        loop(0, 4, split)

        def exchange(i, half=half):
            lo = jnp.dot(Lh[...], Wd[i], preferred_element_type=F32).reshape(16, 8, 256)
            hi = jnp.dot(Lh[...], Wd[2 + i], preferred_element_type=F32).reshape(16, 8, 256)
            both = jnp.concatenate([lo, hi], axis=1)
            eight = pl.ds(8 * half, 8)
            EXs[i, eight] = both[:8].astype(BF16)
            rcopy(EXs.at[i, eight], EXr.at[i, eight], e1s.at[half, i], e1r.at[half, i], other).start()
            Pown[i, eight] = both[8:]

        loop(0, 2, exchange)

        for i in range(2):
            wait_bytes(EXr.at[i, pl.ds(8 * half, 8)], e1r.at[half, i])

            def outward(q, half=half, i=i):
                at = 8 * half + q
                d = lax.rem(at - z + 16, 16)
                to = jnp.where(d < 4, d, jnp.where(d < 8, d - 4, jnp.where(d < 12, d + 4, d)))
                to = jnp.where(d == 8, 4 if i == 0 else 12, to)

                @pl.when(jnp.logical_or(lax.rem(d, 4) != 0, d == 8))
                def _():
                    SB[i, d] = block(at, i).astype(BF16)
                    rcopy(SB.at[i, d], G.at[i, d], e2s.at[i], e2r.at[i, d], zdev(to)).start()

            loop(0, 8, outward)

    sends = []
    for i in range(2):
        for d in (8, 7, 9, 6, 10, 5, 11):
            wait_bytes(G.at[i, d], e2r.at[i, d])
        for side, way in ((0, 1), (1, -1)):
            total = block(chip_at(4 * way), i)
            for d in ((5, 6, 7), (9, 10, 11))[side]:
                total = total + G[i, d].astype(F32)
            if i == side:
                total = total + G[i, 8].astype(F32)
            T4[i, side] = total.astype(BF16)
            cp = rcopy(T4.at[i, side], Fr.at[i, side], e3s.at[i, side], e3r.at[i, side], zdev(4 * way))
            cp.start()
            sends.append(cp)

    totals = []
    for i in range(2):
        total = block(z, i)
        for d in (1, 2, 3, 13, 14, 15):
            wait_bytes(G.at[i, d], e2r.at[i, d])
            total = total + G[i, d].astype(F32)
        totals.append(total)
    for cp in sends:
        cp.wait_send()
    for i in range(2):
        wait_bytes(G.at[i, pl.ds(0, 13)], e2s.at[i])
        for half in range(2):
            wait_bytes(EXs.at[i, pl.ds(8 * half, 8)], e1s.at[half, i])
    wait_bytes(R.at[:, pl.ds(0, NH - 1)], dsd)
    for i in range(2):
        for side in range(2):
            wait_bytes(Fr.at[i, side], e3r.at[i, side])
        total = totals[i] + Fr[i, 0].astype(F32) + Fr[i, 1].astype(F32)
        out[:, 256 * i:256 * i + 256] = total[:8].astype(BF16)
        out[:, 512 + 256 * i:768 + 256 * i] = total[8:].astype(BF16)


def body(tok, gw, gs, gz, uw, us, uz, sb, dw, ds, dz):
    vmem = pl.BlockSpec(memory_space=pltpu.VMEM)
    hbm = pl.BlockSpec(memory_space=pl.ANY)
    V = pltpu.VMEM
    D = pltpu.SemaphoreType.DMA
    operands = (tok, gw, gs, gz, uw, us, uz, sb.reshape(10, 128), dw, ds, dz)
    return pl.pallas_call(
        kernel,
        out_shape=jax.ShapeDtypeStruct((8, 1024), BF16),
        in_specs=[hbm] * 11,
        out_specs=vmem,
        scratch_shapes=[
            *[V(x.shape, x.dtype) for x in operands],
            V((8, 1280), F32), V((8, 1280), F32), V((8, 1280), F32), V((8, 1280), F32),
            V((10, 1, 1024), F32), V((10, 1, 1024), F32), V((10, 1, 128), F32),
            V((10, 1024, 256), BF16),
            V((4, 1280, 256), BF16),
            V((16, 2, 4, 16, 128), BF16),
            V((128, 1024), BF16),
            V((16, 10, 2, 16, 128), BF16),
            V((10, 16, 2, 16, 128), BF16),
            V((10, 16, 128), BF16),
            V((32, 16, 128), BF16),
            V((32, 16, 128), BF16),
            V((10, 16, 128), BF16),
            V((10, 16, 16, 128), BF16),
            V((128, 1280), BF16),
            V((2, 16, 16, 256), BF16), V((2, 16, 16, 256), BF16),
            V((2, 16, 16, 256), F32),
            V((2, 16, 16, 256), BF16), V((2, 16, 16, 256), BF16),
            V((2, 2, 16, 256), BF16), V((2, 2, 16, 256), BF16),
            D((11,)), D((8,)), D((8,)), D, D((18,)), D((16,)), D, D((10,)),
            D((20,)), D, D, D((10,)), D, D((2,)), D((2, 2)), D((2, 2)), D((2,)), D((2, 16)), D((2, 2)), D((2, 2)),
        ],
        compiler_params=pltpu.CompilerParams(
            collective_id=0, has_side_effects=True, vmem_limit_bytes=60 * 1024 * 1024
        ),
        name="rotated_ffn",
    )(*operands)


def solution(mesh):
    in_specs = (
        P("inter", "hid"),
        P("hid", "inter"),
        P("hid", "inter"),
        P("hid", "inter"),
        P("hid", "inter"),
        P("hid", "inter"),
        P("hid", "inter"),
        P("inter"),
        P("inter", "hid"),
        P("inter", "hid"),
        P("inter", "hid"),
    )
    return jax.shard_map(
        body, mesh=mesh, in_specs=in_specs, out_specs=P("inter", "hid"), check_vma=False
    )
```

```python
import functools

import jax
import jax.numpy as jnp
from jax import lax
from jax.experimental import pallas as pl
from jax.experimental.pallas import tpu as pltpu
from jax.sharding import PartitionSpec as P

MESH = pl.DeviceIdType.MESH
F32 = jnp.float32
BF16 = jnp.bfloat16
NH, NZ, NJ, NB = 16, 16, 32, 10


def slot_of(d):
    return (d + 3) % 16


def wait_bytes(view, sem):
    pltpu.make_async_copy(view, view, sem).wait()


def loop(lo, hi, fn):
    def step(i, carry):
        fn(i)
        return carry

    lax.fori_loop(lo, hi, step, 0)


def dequantized(words, zero, scale):
    w = words.astype(jnp.int32)
    planes = []
    for k in range(4):
        d = jnp.right_shift(w, 4 * k) if k else w
        if k < 3:
            d = jnp.bitwise_and(d, 15)
        planes.append(((d.astype(F32) - zero) * scale).astype(BF16))
    return planes


def kernel(
    *refs,
):
    inputs, out, scratch = refs[:11], refs[11], refs[12:]
    held = scratch[:11]
    tok, gw, gs, gz, uw, us, uz, sb, dw, ds, dz = held
    (
    gsf, gzf, usf, uzf, dsf, dzf, sgn,
    W, Wd, X, L, S, B, U, C1, C2, R2, R, Lh, EXs, EXr, Pown, SB, G, T4, Fr,
    w_sem, as1, as2, asc, ar, arc, bs, br, c1s, c1r, c2s, c2r, dsd, drv, e1s, e1r, e2s, e2r, e3s, e3r,
    ) = scratch[11:]
    h = lax.axis_index("hid")
    j = lax.axis_index("inter")
    z = lax.div(j, 2)
    c = lax.rem(j, 2)
    oc = 1 - c

    def zdev(d):
        return (h, 2 * lax.rem(z + d + 16, 16) + c)

    other = (h, 2 * z + oc)

    def rcopy(src, dst, ss, rs, dev):
        return pltpu.make_async_remote_copy(
            src_ref=src, dst_ref=dst, send_sem=ss, recv_sem=rs, device_id=dev, device_id_type=MESH
        )

    near = (4, -4, 3, -3, 2, -2, 1, -1)
    bar = pltpu.get_barrier_semaphore()
    for d in near:
        pl.semaphore_signal(bar, inc=1, device_id=zdev(d), device_id_type=MESH)
    pl.semaphore_signal(bar, inc=1, device_id=other, device_id_type=MESH)
    loop(1, NH, lambda i: pl.semaphore_signal(
        bar, inc=1, device_id=(lax.rem(h + i, NH), j), device_id_type=MESH))

    loads = [pltpu.make_async_copy(inputs[i], held[i], w_sem.at[i]) for i in range(11)]
    for i in (0, 1, 4, 2, 3, 5, 6, 8, 7, 9, 10):
        loads[i].start()

    rows = lax.broadcasted_iota(jnp.int32, (128, 128), 0)
    cols = lax.broadcasted_iota(jnp.int32, (128, 128), 1)
    place = 32 * jnp.bitwise_and(rows, 3) + jnp.right_shift(rows, 2)
    shuffle = jnp.where(place == cols, 1.0, 0.0).astype(BF16)
    def dequant_gu(b):
        at = pl.ds(pl.multiple_of(b * 128, 128), 128)
        for words, zf, sf, lane in ((gw, gzf, gsf, 0), (uw, uzf, usf, 128)):
            for g in range(8):
                planes = dequantized(words[32 * g:32 * g + 32, at], zf[g:g + 1, at], sf[g:g + 1, at])
                for k in range(4):
                    W[b, 128 * g + 32 * k:128 * g + 32 * k + 32, lane:lane + 128] = planes[k]

    loads[0].wait()
    for g in range(4):
        both = [
            jnp.dot(tok[:, 512 * u + 128 * g:512 * u + 128 * g + 128], shuffle, preferred_element_type=F32)
            for u in range(2)
        ]
        X[3, c, g] = jnp.concatenate(both, axis=0).astype(BF16)

    for i in (1, 2, 3, 4, 5, 6):
        loads[i].wait()
    gsf[...] = gs[...].astype(F32)
    usf[...] = us[...].astype(F32)
    gzf[...] = gz[...].astype(F32)
    uzf[...] = uz[...].astype(F32)
    loop(0, 4, dequant_gu)

    pl.semaphore_wait(bar, len(near) + 1 + NH - 1)

    stage1 = [
        rcopy(X.at[3, c], X.at[slot_of(-e), c], as1.at[k], ar.at[slot_of(-e)], zdev(e))
        for k, e in enumerate(near)
    ]
    for cp in stage1:
        cp.start()

    def to_core(s):
        return rcopy(X.at[s, c], X.at[s, c], asc, arc.at[s], other)

    to_core(3).start()
    loop(4, NB, dequant_gu)

    def arrived(s):
        wait_bytes(X.at[s, c], ar.at[s])

    stage2 = []
    for way in (1, -1):
        s = slot_of(-4 * way)
        arrived(s)
        half = 0 if way == 1 else 1
        stage2.append(rcopy(
            X.at[s, c, pl.ds(2 * half, 2)], X.at[slot_of(8), c, pl.ds(2 * half, 2)],
            as2.at[len(stage2)], ar.at[16 + half], zdev(4 * way)))
        for e in (3, 2, 1):
            to = slot_of(-(4 + e) * way)
            stage2.append(rcopy(X.at[s, c], X.at[to, c], as2.at[len(stage2)], ar.at[to], zdev(e * way)))
        for cp in stage2[-4:]:
            cp.start()
    to_core(slot_of(4)).start()
    for e in (1, -1, 2, -2, 3, -3):
        arrived(slot_of(e))
        to_core(slot_of(e)).start()
    to_core(slot_of(-4)).start()

    def products(slots):
        for s in slots:
            wait_bytes(X.at[s, oc], arc.at[s])
        for i, s in enumerate(slots):
            for g in range(4):
                t0, t1 = X[s, 0, g].astype(F32), X[s, 1, g].astype(F32)
                at = slice(16 * i, 16 * i + 16)
                L[at, 128 * g:128 * g + 128] = jnp.concatenate([t0[:8], t1[:8]], axis=0).astype(BF16)
                L[at, 512 + 128 * g:640 + 128 * g] = jnp.concatenate([t0[8:], t1[8:]], axis=0).astype(BF16)

        def product(b):
            v = jnp.dot(L[:16 * len(slots)], W[b], preferred_element_type=F32).astype(BF16)
            for i, s in enumerate(slots):
                n = 10 * lax.rem(z + 13 + s, 16) + b
                m, to = lax.div(n, 16), lax.rem(n, 16)
                for u in range(2):
                    S[s, b, u] = v[16 * i:16 * i + 16, 128 * u:128 * u + 128]

                @pl.when(to != h)
                def _(s=s, m=m, to=to):
                    rcopy(S.at[s, b], B.at[m, h], bs, br.at[m], (to, j)).start()

                @pl.when(to == h)
                def _(s=s, m=m):
                    B[m, h] = S[s, b]

        loop(0, NB, lambda i: product(lax.rem(i + h, NB)))

    products(range(8))
    for e in (5, -5, 6):
        arrived(slot_of(e))
        to_core(slot_of(e)).start()
    for e in (-6, 7, -7):
        arrived(slot_of(e))
        to_core(slot_of(e)).start()
    for half in range(2):
        wait_bytes(X.at[slot_of(8), c, pl.ds(2 * half, 2)], ar.at[16 + half])
    to_core(slot_of(8)).start()
    products((8, 9, 14, 15))
    products((10, 11, 12, 13))

    for i in (7, 8, 9, 10):
        loads[i].wait()
    dsv, dzv, sgv = ds[...].astype(F32), dz[...].astype(F32), (1 - 2 * sb[...]).astype(F32)
    for b in range(NB):
        dsf[b], dzf[b], sgn[b] = dsv[b:b + 1], dzv[b:b + 1], sgv[b:b + 1]

    def dequant_d(b):
        at = pl.ds(pl.multiple_of(b * 32, 32), 32)
        for q in range(8):
            lanes = slice(128 * q, 128 * q + 128)
            planes = dequantized(dw[at, lanes], dzf[b, :, lanes], dsf[b, :, lanes])
            for k in range(4):
                to = pl.ds(pl.multiple_of(b * 128 + 32 * k, 32), 32)
                Wd[q // 2, to, 128 * (q % 2):128 * (q % 2) + 128] = planes[k]

    loop(0, NB, dequant_d)

    for cp in stage1 + stage2:
        cp.wait_send()
    wait_bytes(X.at[:, c], asc)

    def owner_of(m, side):
        return 8 * lax.div(m, 5) + lax.rem(m, 5) + 16 * side

    def collect(m):
        for side in range(2):
            owner = owner_of(m, side)

            @pl.when(owner != j)
            def _():
                rcopy(U.at[m], C1.at[j], c1s.at[2 * m + side], c1r, (h, owner)).start()

            @pl.when(owner == j)
            def _():
                C1[j] = U[m]

    n0 = 10 * lax.rem(z + 13, 16)
    n0 = n0 + lax.rem(h - n0 + 160, 16)

    def unit(k):
        n = lax.rem(n0 + 16 * k, 160)
        m = lax.div(n, 16)
        wait_bytes(B.at[m, pl.ds(0, NH - 1)], br.at[m])
        total = B[m, 0].astype(F32)
        for s in range(1, NH):
            total = total + B[m, s].astype(F32)
        gate, up = total[0], total[1]
        hidden = gate / (1.0 + jnp.exp(-gate)) * up
        U[m] = (hidden * sgn[lax.rem(n, 10)]).astype(BF16)
        collect(m)

    loop(0, 5, unit)
    loop(0, 5, lambda i: unit(5 + (4 * lax.rem(i, 2)) + lax.div(i, 2) * (1 - 2 * lax.rem(i, 2))))

    owns = lax.rem(j, 8) < 5
    mine = 5 * lax.div(lax.rem(j, 16), 8) + lax.rem(j, 8)

    @pl.when(owns)
    def _():
        turned = 4 * jnp.bitwise_and(cols, 31) + jnp.right_shift(cols, 5)
        common = jnp.bitwise_and(rows, turned)
        odd = jnp.zeros_like(common)
        for bit in range(7):
            odd = jnp.bitwise_xor(odd, jnp.right_shift(common, bit))
        factor = (1 - 2 * jnp.bitwise_and(odd, 1)).astype(F32).astype(BF16)
        wait_bytes(C1.at[pl.ds(0, NJ - 1)], c1r)
        vals = [jnp.dot(C1[i], factor, preferred_element_type=F32) for i in range(NJ)]
        step = 1
        while step < NJ:
            vals = [
                vals[i] + vals[i ^ step] if not i & step else vals[i ^ step] - vals[i] for i in range(NJ)
            ]
            step *= 2
        for i in range(NJ):
            C2[i] = (vals[i] * (1.0 / 64.0)).astype(BF16)

        def back(q):
            d = lax.div(q + 2, 4)
            d = jnp.where(lax.rem(lax.div(q, 2), 2) == 0, d - 4, 4 - d)
            i = 2 * lax.rem(z + d + 16, 16) + lax.rem(q, 2)

            @pl.when(i != j)
            def _():
                rcopy(C2.at[i], R2.at[mine], c2s, c2r.at[mine], (h, i)).start()

        loop(0, 16, back)
        R2[mine] = C2[j]

    first_half = lax.rem(lax.div(z + 1, 4), 2)
    rising = lax.rem(z + 1, 4) < 2
    for step in range(NB):
        half = first_half if step < 5 else 1 - first_half
        m = 5 * half + jnp.where(rising, step % 5, 4 - step % 5)

        @pl.when(jnp.logical_not(jnp.logical_and(owns, m == mine)))
        def _(m=m):
            wait_bytes(R2.at[m], c2r.at[m])

        def spread(p, m=m, half=half):
            y = lax.rem(lax.div(h, 4) + lax.div(p + 10, 4), 4)
            x = lax.rem(h + p + 10, 4)
            rcopy(R2.at[m], R.at[m, h], dsd, drv.at[half], (4 * y + x, j)).start()

        loop(0, 6, spread)
        loop(7, NH, spread)
        R[m, h] = R2[m]

    wait_bytes(S.at[pl.ds(0, 15)], bs)

    def collected(m):
        for side in range(2):
            @pl.when(owner_of(m, side) != j)
            def _():
                wait_bytes(U.at[m], c1s.at[2 * m + side])

    loop(0, NB, collected)

    @pl.when(owns)
    def _():
        wait_bytes(C2.at[pl.ds(0, 15)], c2s)

    def block(at, i):
        return Pown[i, at] + EXr[i, at].astype(F32)

    def chip_at(d):
        return lax.rem(z + d + 16, 16)

    for half in (first_half, 1 - first_half):
        wait_bytes(R.at[pl.ds(5 * half, 5), pl.ds(0, NH - 1)], drv.at[half])

        def split(a, half=half):
            for b in range(NB):
                n = 80 * half + 20 * a + b
                t0 = R[lax.div(n, 16), lax.rem(n, 16)].astype(F32)
                t1 = R[lax.div(n + 10, 16), lax.rem(n + 10, 16)].astype(F32)
                low = jnp.concatenate([t0[:8], t1[:8]], axis=0)
                high = jnp.concatenate([t0[8:], t1[8:]], axis=0)
                lanes = slice(128 * b, 128 * b + 128)
                at = pl.multiple_of(16 * a, 16)
                Lh[pl.ds(at, 16), lanes] = jnp.where(c == 0, high, low).astype(BF16)
                Lh[pl.ds(at + 64, 16), lanes] = jnp.where(c == 0, low, high).astype(BF16)

        loop(0, 4, split)

        def exchange(i, half=half):
            lo = jnp.dot(Lh[...], Wd[i], preferred_element_type=F32).reshape(16, 8, 256)
            hi = jnp.dot(Lh[...], Wd[2 + i], preferred_element_type=F32).reshape(16, 8, 256)
            both = jnp.concatenate([lo, hi], axis=1)
            eight = pl.ds(8 * half, 8)
            EXs[i, eight] = both[:8].astype(BF16)
            rcopy(EXs.at[i, eight], EXr.at[i, eight], e1s.at[half, i], e1r.at[half, i], other).start()
            Pown[i, eight] = both[8:]

        loop(0, 2, exchange)

        for i in range(2):
            wait_bytes(EXr.at[i, pl.ds(8 * half, 8)], e1r.at[half, i])

            def outward(q, half=half, i=i):
                at = 8 * half + q
                d = lax.rem(at - z + 16, 16)
                to = jnp.where(d < 4, d, jnp.where(d < 8, d - 4, jnp.where(d < 12, d + 4, d)))
                to = jnp.where(d == 8, 4 if i == 0 else 12, to)

                @pl.when(jnp.logical_or(lax.rem(d, 4) != 0, d == 8))
                def _():
                    SB[i, d] = block(at, i).astype(BF16)
                    rcopy(SB.at[i, d], G.at[i, d], e2s.at[i], e2r.at[i, d], zdev(to)).start()

            loop(0, 8, outward)

    sends = []
    for i in range(2):
        for d in (8, 7, 9, 6, 10, 5, 11):
            wait_bytes(G.at[i, d], e2r.at[i, d])
        for side, way in ((0, 1), (1, -1)):
            total = block(chip_at(4 * way), i)
            for d in ((5, 6, 7), (9, 10, 11))[side]:
                total = total + G[i, d].astype(F32)
            if i == side:
                total = total + G[i, 8].astype(F32)
            T4[i, side] = total.astype(BF16)
            cp = rcopy(T4.at[i, side], Fr.at[i, side], e3s.at[i, side], e3r.at[i, side], zdev(4 * way))
            cp.start()
            sends.append(cp)

    totals = []
    for i in range(2):
        total = block(z, i)
        for d in (1, 2, 3, 13, 14, 15):
            wait_bytes(G.at[i, d], e2r.at[i, d])
            total = total + G[i, d].astype(F32)
        totals.append(total)
    for cp in sends:
        cp.wait_send()
    for i in range(2):
        wait_bytes(G.at[i, pl.ds(0, 13)], e2s.at[i])
        for half in range(2):
            wait_bytes(EXs.at[i, pl.ds(8 * half, 8)], e1s.at[half, i])
    wait_bytes(R.at[:, pl.ds(0, NH - 1)], dsd)
    for i in range(2):
        for side in range(2):
            wait_bytes(Fr.at[i, side], e3r.at[i, side])
        total = totals[i] + Fr[i, 0].astype(F32) + Fr[i, 1].astype(F32)
        out[:, 256 * i:256 * i + 256] = total[:8].astype(BF16)
        out[:, 512 + 256 * i:768 + 256 * i] = total[8:].astype(BF16)


def body(tok, gw, gs, gz, uw, us, uz, sb, dw, ds, dz):
    vmem = pl.BlockSpec(memory_space=pltpu.VMEM)
    hbm = pl.BlockSpec(memory_space=pl.ANY)
    V = pltpu.VMEM
    D = pltpu.SemaphoreType.DMA
    operands = (tok, gw, gs, gz, uw, us, uz, sb.reshape(10, 128), dw, ds, dz)
    return pl.pallas_call(
        kernel,
        out_shape=jax.ShapeDtypeStruct((8, 1024), BF16),
        in_specs=[hbm] * 11,
        out_specs=vmem,
        scratch_shapes=[
            *[V(x.shape, x.dtype) for x in operands],
            V((8, 1280), F32), V((8, 1280), F32), V((8, 1280), F32), V((8, 1280), F32),
            V((10, 1, 1024), F32), V((10, 1, 1024), F32), V((10, 1, 128), F32),
            V((10, 1024, 256), BF16),
            V((4, 1280, 256), BF16),
            V((16, 2, 4, 16, 128), BF16),
            V((128, 1024), BF16),
            V((16, 10, 2, 16, 128), BF16),
            V((10, 16, 2, 16, 128), BF16),
            V((10, 16, 128), BF16),
            V((32, 16, 128), BF16),
            V((32, 16, 128), BF16),
            V((10, 16, 128), BF16),
            V((10, 16, 16, 128), BF16),
            V((128, 1280), BF16),
            V((2, 16, 16, 256), BF16), V((2, 16, 16, 256), BF16),
            V((2, 16, 16, 256), F32),
            V((2, 16, 16, 256), BF16), V((2, 16, 16, 256), BF16),
            V((2, 2, 16, 256), BF16), V((2, 2, 16, 256), BF16),
            D((11,)), D((8,)), D((8,)), D, D((18,)), D((16,)), D, D((10,)),
            D((20,)), D, D, D((10,)), D, D((2,)), D((2, 2)), D((2, 2)), D((2,)), D((2, 16)), D((2, 2)), D((2, 2)),
        ],
        compiler_params=pltpu.CompilerParams(
            collective_id=0, has_side_effects=True, vmem_limit_bytes=60 * 1024 * 1024
        ),
        name="rotated_ffn",
    )(*operands)


def solution(mesh):
    in_specs = (
        P("inter", "hid"),
        P("hid", "inter"),
        P("hid", "inter"),
        P("hid", "inter"),
        P("hid", "inter"),
        P("hid", "inter"),
        P("hid", "inter"),
        P("inter"),
        P("inter", "hid"),
        P("inter", "hid"),
        P("inter", "hid"),
    )
    return jax.shard_map(
        body, mesh=mesh, in_specs=in_specs, out_specs=P("inter", "hid"), check_vma=False
    )
```
